1024 devices in a mesh: outer: 4 (over x), dp: 32 (over z, core), tensor: 8 (over y).
Axes of the slice: x: 4, y: 8, z: 16, core: 2. Of those that a mesh axis runs over, the one named last changes fastest.
Arguments:
- tokens: bfloat16 [49152, 1024], P(('outer', 'dp'), 'tensor'), may hold values from -8 to 8
- input_weight: bfloat16 [1024, 3, 1024], P(None, None, 'tensor'), may hold values from -1 to 1
- output_weight: bfloat16 [1024, 1024], P('tensor'), may hold values from -0.1875 to 0.1875
- grad_layer: bfloat16 [49152, 1024], P(('outer', 'dp'), 'tensor'), may hold values from -6 to 6
- patch_blocks: int32 [128, 3], replicated, may hold values from 1 to 2, as said below
- target_group: int32 [128, 3], replicated, may hold values from 0 to 31, as said below
Outputs:
- layer_out: bfloat16 [49152, 1024], P(('outer', 'dp'), 'tensor')
- grad_tokens: bfloat16 [49152, 1024], P(('outer', 'dp'), 'tensor')
- grad_input_weight: float32 [1024, 3, 1024], P(None, None, 'tensor')
- grad_output_weight: float32 [1024, 1024], P('tensor')
The draws below stay inside these ranges and needn't reach their ends.
Inputs may be any that keep to these rules, and one draw needn't show every extreme that they name: Image i of group g has 64 * patch_blocks[g, i] patches; a group's images lie one after another from its first row. `target_group`: the index along dp of the group that takes image i of group g, within g's index along outer. A group hands at most one image to other groups and takes at most one from them, and after the moves each group's images fit in 384 rows.
All inputs are finite; a program needn't handle non-finite values.
Results may differ from the reference program's by a relative error of at most 0.02.
Values may be sent and summed in bfloat16 or wider, within the bound.
A program may use at most 32 MiB of HBM per device.

```python
import jax
import jax.numpy as jnp
from jax import lax

D = 1024
HEADS = 16
BLOCK = 64
LEN_MAX = 2
IMG = 3
ROWS = 384
GROUPS = 128
N_DP = 32
N_TENSOR = 8


def move_plan(key):
    key = jax.random.fold_in(key, 11)
    key_length, key_turn = jax.random.split(key)
    outer_count = GROUPS // N_DP
    half = N_DP // 2
    blocks = jax.random.randint(key_length, (outer_count, N_DP, IMG), 1, LEN_MAX + 1, dtype=jnp.int32)
    turns = jax.random.randint(key_turn, (outer_count, 1), 0, N_DP, dtype=jnp.int32)
    devices = jnp.broadcast_to(jnp.arange(N_DP, dtype=jnp.int32)[None, :], (outer_count, N_DP))
    relative = (devices - turns) % N_DP
    heaviest = relative == 0
    lightest = relative == half + 1
    sender_mid = relative == half
    sender_next = relative == 1
    sending = heaviest | sender_mid | sender_next
    blocks = jnp.where(heaviest[..., None], LEN_MAX, blocks)
    blocks = jnp.where(lightest[..., None], 1, blocks)
    last_index = jnp.arange(IMG, dtype=jnp.int32)[None, None, :] == IMG - 1
    blocks = jnp.where(sending[..., None] & last_index, LEN_MAX, blocks).astype(jnp.int32)
    partner = jnp.where(heaviest, (devices + half) % N_DP, jnp.where(sender_mid, (devices + 1) % N_DP, jnp.where(sender_next, (devices - 1) % N_DP, devices))).astype(jnp.int32)
    dest = jnp.broadcast_to(devices[..., None], (outer_count, N_DP, IMG))
    dest = jnp.where(last_index, partner[..., None], dest).astype(jnp.int32)
    return (blocks.reshape(GROUPS, IMG), dest.reshape(GROUPS, IMG))


def draw_patch_blocks(key, part):
    blocks, dest = move_plan(key)
    return blocks


def draw_target_group(key, part):
    blocks, dest = move_plan(key)
    return dest


def draw_tokens(key, part):
    key = jax.random.fold_in(key, 3)
    first = jax.random.fold_in(key, 0)
    total_rows = GROUPS * ROWS
    values = jnp.clip(jax.random.normal(first, (total_rows, D), jnp.float32), -8.0, 8.0)
    return values.astype(jnp.bfloat16)


def draw_input_weight(key, part):
    key = jax.random.fold_in(key, 5)
    first = jax.random.fold_in(key, 0)
    raw = jax.random.normal(first, (D, 3, D), jnp.float32) * D ** (-0.5)
    return jnp.clip(raw, -1.0, 1.0).astype(jnp.bfloat16)


def level_of(own_key, extent, pieces, low, high):
    def one(dim, parts):
        steps = jax.random.uniform(jax.random.fold_in(jax.random.fold_in(own_key, 6), dim), (parts,), jnp.float32, low / len(pieces), high / len(pieces))
        return jnp.repeat(jnp.exp(steps), extent[dim] // parts).reshape((-1,) + (1,) * (len(extent) - dim - 1))

    gain = one(*pieces[0])
    for cut in pieces[1:]:
        gain = gain * one(*cut)
    return gain


def noise(key, shape, spread, limit, cuts=(), kind=jnp.bfloat16):
    values = jax.random.normal(key, shape, jnp.float32) * spread
    if len(cuts) > 0:
        values = level_of(key, shape, cuts, -0.22, 0.18) * values
    return jnp.clip(values, min=-limit, max=limit).astype(kind)


def setup_inputs(seed: int = 0) -> dict:
    streams_of = jax.random.split(jax.random.key(seed), 7)
    return {
        "tokens": draw_tokens(jax.random.fold_in(streams_of[6], 71), 0),
        "input_weight": draw_input_weight(jax.random.fold_in(streams_of[6], 71), 0),
        "output_weight": noise(streams_of[2], (D, D), D ** -0.5, 0.1875, ((0, 8),)),
        "grad_layer": noise(streams_of[3], (GROUPS * ROWS, D), 1.0, 6.0, ((0, 128), (1, 8))),
        "patch_blocks": draw_patch_blocks(jax.random.fold_in(streams_of[6], 71), 0),
        "target_group": draw_target_group(jax.random.fold_in(streams_of[6], 71), 0),
    }


def layout(group_blocks, group_dest, place, row_count, capacity):
    group_count, image_count = group_blocks.shape
    sources = jnp.arange(group_count, dtype=jnp.int32)
    picked = (sources == place)[:, None]
    lens_all = (BLOCK * group_blocks).astype(jnp.int32)
    starts_all = (jnp.cumsum(lens_all, axis=1) - lens_all).astype(jnp.int32)
    own_len = jnp.sum(jnp.where(picked, lens_all, 0), axis=0).astype(jnp.int32)
    own_start = jnp.sum(jnp.where(picked, starts_all, 0), axis=0).astype(jnp.int32)
    own_dest = jnp.sum(jnp.where(picked, group_dest, 0), axis=0).astype(jnp.int32)
    staying = own_dest == place
    kept_len = jnp.where(staying, own_len, 0).astype(jnp.int32)
    dst_off = (jnp.cumsum(kept_len) - kept_len).astype(jnp.int32)
    kept_total = jnp.sum(kept_len).astype(jnp.int32)
    out_len = jnp.sum(jnp.where(staying, 0, own_len)).astype(jnp.int32)
    out_start = jnp.sum(jnp.where(staying, 0, own_start)).astype(jnp.int32)
    target_peer = jnp.sum(jnp.where(staying, 0, own_dest)).astype(jnp.int32)
    coming = (group_dest == place) & (group_dest != sources[:, None])
    in_len = jnp.sum(jnp.where(coming, lens_all, 0)).astype(jnp.int32)
    source_peer = jnp.sum(jnp.where(coming, sources[:, None], 0)).astype(jnp.int32)
    in_start = jnp.sum(jnp.where(coming, starts_all, 0)).astype(jnp.int32)
    seg_off = jnp.concatenate([dst_off, kept_total[None]]).astype(jnp.int32)
    seg_len = jnp.concatenate([kept_len, in_len[None]]).astype(jnp.int32)
    position = jnp.arange(row_count, dtype=jnp.int32)
    inside = (position[:, None] >= seg_off[None, :]) & (position[:, None] < (seg_off + seg_len)[None, :])
    segment_marks = jnp.arange(image_count + 1, dtype=jnp.int32)
    segment = jnp.sum(jnp.where(inside, segment_marks[None, :], 0), axis=1).astype(jnp.int32)
    live = jnp.any(inside, axis=1)
    offset_in = (position - jnp.sum(jnp.where(inside, seg_off[None, :], 0), axis=1)).astype(jnp.int32)
    own_src = jnp.sum(jnp.where(inside[:, :image_count], own_start[None, :], 0), axis=1).astype(jnp.int32)
    pull = jnp.where(segment < image_count, own_src + offset_in, row_count + offset_in)
    pull = jnp.where(live, pull, row_count + capacity).astype(jnp.int32)
    own_inside = (position[:, None] >= own_start[None, :]) & (position[:, None] < (own_start + own_len)[None, :])
    target = jnp.where(staying, dst_off - own_start, row_count - own_start)
    back = position + jnp.sum(jnp.where(own_inside, target[None, :], 0), axis=1)
    back = jnp.where(jnp.any(own_inside, axis=1), back, row_count + capacity).astype(jnp.int32)
    slot_index = jnp.arange(capacity, dtype=jnp.int32)
    send = jnp.where(slot_index < out_len, out_start + slot_index, row_count).astype(jnp.int32)
    reply = jnp.where(slot_index < in_len, kept_total + slot_index, row_count).astype(jnp.int32)
    block_ok = slot_index[None, :] < seg_len[:, None]
    block_rows = jnp.where(block_ok, seg_off[:, None] + slot_index[None, :], row_count).astype(jnp.int32)
    flat_back = jnp.where(live, segment * capacity + offset_in, (image_count + 1) * capacity).astype(jnp.int32)
    return {"segment": segment, "live": live, "offset_in": offset_in, "own_src": own_src, "pull": pull,
            "back": back, "send": send, "reply": reply, "block_ok": block_ok, "block_rows": block_rows,
            "flat_back": flat_back, "out_len": out_len, "in_len": in_len, "target_peer": target_peer,
            "source_peer": source_peer, "in_start": in_start}


def attend(queries, key_rows, value_rows, allowed, row_ok):
    scores = jnp.einsum("blhd,bmhd->bhlm", queries.astype(jnp.float32), key_rows.astype(jnp.float32)) * 0.125
    allowed_heads = allowed[:, None]
    scores = jnp.where(allowed_heads, scores, -1e30)
    row_peak = jnp.max(scores, axis=-1, keepdims=True)
    weights = jnp.exp(scores - row_peak) * allowed_heads.astype(jnp.float32)
    totals = jnp.sum(weights, axis=-1, keepdims=True)
    totals = jnp.where(row_ok[:, None, :, None], totals, 1.0)
    shares = weights / totals
    shares_low = shares.astype(jnp.bfloat16)
    attended = jnp.einsum("bhlm,bmhd->blhd", shares_low.astype(jnp.float32), value_rows.astype(jnp.float32))
    return attended.astype(jnp.bfloat16), shares, shares_low


def attend_back(queries, key_rows, value_rows, shares, shares_low, grad_attended):
    grad_shares = jnp.einsum("blhd,bmhd->bhlm", grad_attended.astype(jnp.float32), value_rows.astype(jnp.float32))
    inner_sum = jnp.sum(shares * grad_shares, axis=-1, keepdims=True)
    grad_scores = (0.125 * shares * (grad_shares - inner_sum)).astype(jnp.bfloat16)
    grad_query = jnp.einsum("bhlm,bmhd->blhd", grad_scores.astype(jnp.float32), key_rows.astype(jnp.float32))
    grad_key = jnp.einsum("bhlm,blhd->bmhd", grad_scores.astype(jnp.float32), queries.astype(jnp.float32))
    grad_value = jnp.einsum("bhlm,blhd->bmhd", shares_low.astype(jnp.float32), grad_attended.astype(jnp.float32))
    return jnp.stack([grad_query.astype(jnp.bfloat16), grad_key.astype(jnp.bfloat16),
                      grad_value.astype(jnp.bfloat16)], axis=2)


def reference(tokens, input_weight, output_weight, grad_layer, patch_blocks, target_group):
    model_width = D
    narrow = D // N_TENSOR
    head_dim = D // HEADS
    capacity = LEN_MAX * BLOCK
    zero_row = jnp.zeros((1, model_width), jnp.bfloat16)
    padded_tokens = jnp.concatenate([tokens, zero_row])
    flat_weight = input_weight.reshape(model_width, 3 * model_width)
    split_weight = input_weight.reshape(model_width, 3, N_TENSOR, narrow).astype(jnp.float32)
    split_output = output_weight.reshape(N_TENSOR, narrow, model_width).astype(jnp.float32)

    def one_group(sums_carry, group_number):
        outer_place = (group_number // N_DP).astype(jnp.int32)
        group_place = (group_number % N_DP).astype(jnp.int32)
        group_blocks = lax.dynamic_slice_in_dim(patch_blocks, outer_place * N_DP, N_DP, 0)
        group_dest = lax.dynamic_slice_in_dim(target_group, outer_place * N_DP, N_DP, 0)
        arrangement = layout(group_blocks, group_dest, group_place, ROWS, capacity)
        source_row = jnp.where(arrangement["segment"] < IMG,
                               group_number * ROWS + arrangement["own_src"] + arrangement["offset_in"],
                               (outer_place * N_DP + arrangement["source_peer"]) * ROWS
                               + arrangement["in_start"] + arrangement["offset_in"])
        source_row = jnp.where(arrangement["live"], source_row, GROUPS * ROWS).astype(jnp.int32)
        arranged = jnp.take(padded_tokens, source_row, axis=0)
        grad_rows = lax.dynamic_slice_in_dim(grad_layer, group_number * ROWS, ROWS, 0)
        projected = jnp.dot(arranged, flat_weight, preferred_element_type=jnp.float32)
        projected = projected.astype(jnp.bfloat16).reshape(ROWS, 3, HEADS, head_dim)
        segment = arrangement["segment"]
        live = arrangement["live"]
        allowed = ((segment[:, None] == segment[None, :]) & live[:, None] & live[None, :])[None]
        queries = projected[None, :, 0]
        key_rows = projected[None, :, 1]
        value_rows = projected[None, :, 2]
        attended, shares, shares_low = attend(queries, key_rows, value_rows, allowed, live[None])
        attended_rows = attended.reshape(ROWS, N_TENSOR, narrow)
        out_parts = jnp.einsum("rtc,tcd->rtd", attended_rows.astype(jnp.float32), split_output)
        out_parts = lax.optimization_barrier(out_parts.astype(jnp.bfloat16))
        layer_rows = jnp.sum(out_parts.astype(jnp.float32), axis=1).astype(jnp.bfloat16)
        grad_attended = jnp.dot(grad_rows, output_weight.T, preferred_element_type=jnp.float32)
        grad_attended = grad_attended.astype(jnp.bfloat16).reshape(1, ROWS, HEADS, head_dim)
        gradients = attend_back(queries, key_rows, value_rows, shares, shares_low, grad_attended)
        gradients = gradients.reshape(ROWS, 3, N_TENSOR, narrow)
        back_parts = jnp.einsum("rjtc,djtc->rtd", gradients.astype(jnp.float32), split_weight)
        back_parts = lax.optimization_barrier(back_parts.astype(jnp.bfloat16))
        grad_target = jnp.sum(back_parts.astype(jnp.float32), axis=1).astype(jnp.bfloat16)
        term_input = jnp.einsum("rd,rje->dje", arranged.astype(jnp.float32),
                                gradients.reshape(ROWS, 3, model_width).astype(jnp.float32))
        term_output = jnp.einsum("re,rd->ed", attended_rows.reshape(ROWS, model_width).astype(jnp.float32),
                                 grad_rows.astype(jnp.float32))
        return (sums_carry[0] + term_input, sums_carry[1] + term_output), (layer_rows, grad_target, source_row)

    start_sums = (jnp.zeros((model_width, 3, model_width), jnp.float32),
                  jnp.zeros((model_width, model_width), jnp.float32))
    final_sums, stacked = lax.scan(one_group, start_sums, jnp.arange(GROUPS, dtype=jnp.int32))
    layer_out = stacked[0].reshape(GROUPS * ROWS, model_width)
    grad_tokens = jnp.zeros((GROUPS * ROWS + 1, model_width), jnp.bfloat16)
    grad_tokens = grad_tokens.at[stacked[2].reshape(-1)].set(stacked[1].reshape(GROUPS * ROWS, model_width))
    return layer_out, grad_tokens[:-1], final_sums[0], final_sums[1]
```

```python
import jax
import jax.numpy as jnp
from jax import lax
from jax.experimental import pallas as pl
from jax.experimental.pallas import tpu as pltpu
from jax.sharding import PartitionSpec as P

MESH = pl.DeviceIdType.MESH
BF16 = jnp.bfloat16
F32 = jnp.float32

ROWS = 384
NARROW = 128
BLOCK = 64
BLOCKS = 6
IMG = 3
CAP = 128
NT = 8
NZ = 16
NX = 4
NDP = 32
HALF = ROWS // 2
EXTRA = ROWS + CAP
WINDOWS = (0, 64, 128)


def dot(a, b, ca=1, cb=0):
    return lax.dot_general(a, b, (((ca,), (cb,)), ((), ())), preferred_element_type=F32)


def one_if(condition):
    return jnp.where(condition, 1.0, 0.0)


def count(shape, axis):
    return lax.broadcasted_iota(jnp.int32, shape, axis).astype(F32)


def copy_to(src, dst, send, recv, **device):
    return pltpu.make_async_remote_copy(
        src_ref=src,
        dst_ref=dst,
        send_sem=send,
        recv_sem=recv,
        device_id=device,
        device_id_type=MESH,
    )


def kernel(
    tok, wi, wo, gl, pb, tg,
    lay_o, gtok_o, giw_o, gow_o,
    tf, gf, pg, pa, move, qkv, ga, shares, att, attx, gcat, gacc,
    part, csum, crecv, xrecv, tsum, zrecv, full,
    pback, pout, rback, rout,
    ring_s, ring_r, img_s, img_r, zg_s, zg_r, za_s, za_r, sib_s, sib_r,
    core_s, core_r, xr_s, xr_r, zr_s, zr_r, zb_s, zb_r, xb_s, xb_r, cb_s, cb_r,
    rs_s, rs_r,
):
    o = lax.axis_index("outer")
    d = lax.axis_index("dp")
    t = lax.axis_index("tensor")
    z = lax.div(d, 2)
    c = lax.rem(d, 2)
    sibling = d + 1 - 2 * c

    def yat(k):
        return lax.rem(t + (k + NT), NT)

    def zat(k):
        return lax.rem(z + (k + NZ), NZ)

    def xat(k):
        return lax.rem(o + k, NX)

    pending = []

    def go(cp):
        cp.start()
        pending.append(cp)

    barrier = pltpu.get_barrier_semaphore()

    def greet(**device):
        pl.semaphore_signal(barrier, inc=1, device_id=device, device_id_type=MESH)

    for k in range(1, NZ):
        greet(dp=2 * zat(k) + c)
    greet(dp=sibling)
    for k in range(1, NT):
        greet(tensor=yat(k))
    for k in range(1, NX):
        greet(outer=xat(k))

    here = d.astype(F32)
    group = (o * NDP + d).astype(F32)
    lane3 = count((IMG, NARROW), 1)
    blocks_all = pb[...].astype(F32)
    dest_all = tg[...].astype(F32)
    own = one_if(lane3 == group)
    length3 = jnp.sum(blocks_all * own, axis=1, keepdims=True)
    dest3 = jnp.sum(dest_all * own, axis=1, keepdims=True)
    length = [length3[i : i + 1] for i in range(IMG)]
    dest = [dest3[i : i + 1] for i in range(IMG)]
    first = [jnp.zeros((1, 1), F32), length[0], length[0] + length[1]]
    total = first[2] + length[2]
    stays = [one_if(dest[i] == here) for i in range(IMG)]
    moved = [1.0 - stays[i] for i in range(IMG)]
    kept = [stays[i] * length[i] for i in range(IMG)]
    place = [jnp.zeros((1, 1), F32), kept[0], kept[0] + kept[1]]
    kept_total = place[2] + kept[2]
    target = moved[0] * dest[0] + moved[1] * dest[1] + moved[2] * dest[2]

    cut = one_if(count((CAP, ROWS), 1) == count((CAP, ROWS), 0) + BLOCK * kept_total)
    pg[c, z] = dot(cut.astype(BF16), gl[...]).astype(BF16)
    tf[t] = tok[...]
    gf[t, :ROWS, :] = gl[...]

    pl.semaphore_wait(barrier, (NZ - 1) + 1 + (NT - 1) + (NX - 1))

    def gather_z(buf, ss, rs, n):
        def msg(a, j, half=None):
            k = (a + j) % NZ
            sem = NZ if half == 1 else k
            ref = buf.at[c, zat(-a)]
            if half is not None:
                ref = ref.at[pl.ds(half * BLOCK, BLOCK)]
            return copy_to(ref, ref, ss.at[sem], rs.at[sem], dp=2 * zat(j) + c)

        def arrived(k, half=None):
            sem = NZ if half == 1 else k
            ref = buf.at[c, zat(-k)]
            if half is not None:
                ref = ref.at[pl.ds(half * BLOCK, BLOCK)]
            copy_to(ref, ref, ss.at[sem], rs.at[sem], dp=2 * zat(k) + c).wait_recv()

        def one():
            for j in (6, -6, 3, -3, 1, -1):
                go(msg(0, j))

        def two():
            arrived(3)
            go(msg(3, 1))
            go(msg(3, -1))
            arrived(13)
            go(msg(-3, -1))
            go(msg(-3, 1))

        def three():
            arrived(6)
            go(msg(6, 2, 0))
            go(msg(6, 1))
            go(msg(6, -1))
            arrived(10)
            go(msg(-6, -2, 1))
            go(msg(-6, -1))
            go(msg(-6, 1))

        def cross():
            return copy_to(buf.at[c], buf.at[c], sib_s.at[n], sib_r.at[n], dp=sibling)

        def four():
            for k in (1, 15, 2, 14, 4, 12, 5, 11, 7, 9):
                arrived(k)
            arrived(8, 0)
            arrived(8, 1)
            go(cross())

        def five():
            cross().wait_recv()

        return one, two, three, four, five

    zg = gather_z(pg, zg_s, zg_r, 0)
    za = gather_z(pa, za_s, za_r, 1)

    def ring_msg(step, way, buf, n, half):
        slot = yat(-way * (step - 1))
        ref = buf.at[slot, pl.ds(half * HALF, HALF)]
        sem = ((step - 1) * 2 + (way + 1) // 2) * 4 + n * 2 + half
        return copy_to(ref, ref, ring_s.at[sem], ring_r.at[sem], tensor=yat(way))

    def ring_sends(step):
        for half in range(2):
            for n, buf in enumerate((tf, gf)):
                for way in (1, -1):
                    if step < 4 or half == (1 - way) // 2:
                        go(ring_msg(step, way, buf, n, half))

    def ring_waits(step):
        for half in range(2):
            for n, buf in enumerate((tf, gf)):
                for way in (1, -1):
                    if step < 4 or half == (1 - way) // 2:
                        slot = yat(-way * step)
                        ref = buf.at[slot, pl.ds(half * HALF, HALF)]
                        sem = ((step - 1) * 2 + (way + 1) // 2) * 4 + n * 2 + half
                        copy_to(
                            ref, ref, ring_s.at[sem], ring_r.at[sem], tensor=yat(way)
                        ).wait_recv()
                        if step < 3 or (step == 3 and half == (1 - way) // 2):
                            go(ring_msg(step + 1, way, buf, n, half))

    zg[0]()
    ring_sends(1)
    zg[1]()
    ring_waits(1)
    zg[2]()
    ring_waits(2)
    zg[3]()
    zg[4]()

    def pick(buf, peer):
        acc = jnp.zeros((CAP, NARROW), BF16)
        for k in range(NDP):
            mark = jnp.broadcast_to(one_if(peer == float(k)), (1, NARROW)).astype(BF16)
            acc = acc + buf[k % 2, k // 2] * mark
        return acc

    gf[t, ROWS:, :] = pick(pg, target)
    img_ref = gf.at[t, pl.ds(ROWS, CAP)]
    for k in (4, 3, 5, 2, 6, 1, 7):
        go(copy_to(img_ref, img_ref, img_s.at[k], img_r.at[k], tensor=yat(k)))
    ring_waits(3)
    ring_waits(4)

    tokens = jnp.concatenate([tf[n] for n in range(NT)], axis=1)
    for j in range(3):
        qkv[j] = dot(tokens, wi[j]).astype(BF16)

    lane = lax.broadcasted_iota(jnp.int32, (1, NARROW), 1)
    low = lane < BLOCK
    zero = jnp.zeros((), F32)

    def two_heads(x):
        x = x.astype(F32)
        return jnp.concatenate(
            [jnp.where(low, x, zero).astype(BF16), jnp.where(low, zero, x).astype(BF16)], axis=0
        )

    def one_head(x):
        return jnp.where(low, x[:CAP], x[CAP:])

    row = count((ROWS, 1), 0)
    column = jnp.full((ROWS, 1), -1.0, F32)
    for i in range(IMG):
        inside = one_if(row >= BLOCK * first[i]) * one_if(row < BLOCK * (first[i] + length[i]))
        shift = BLOCK * (stays[i] * place[i] + moved[i] * BLOCKS - first[i])
        column = column + inside * (row + shift + 1.0)
    move[...] = one_if(count((ROWS, EXTRA), 1) == column).astype(BF16)

    def image_of(position):
        marks = jnp.zeros(position.shape, F32)
        for edge in (first[1], first[2], total):
            marks = marks + one_if(position >= edge * BLOCK)
        return marks

    for i, start in enumerate(WINDOWS):
        place_in = count((2 * CAP, 1), 0)
        row_image = image_of(place_in - CAP * one_if(place_in >= CAP) + i * CAP)
        key_image = image_of(count((1, 2 * CAP), 1) + start)
        allowed = (row_image == key_image) & (row_image < IMG)
        query = two_heads(qkv[0, i * CAP : (i + 1) * CAP, :])
        scores = dot(query, qkv[1, start : start + 2 * CAP, :], 1, 1) * 0.125
        scores = jnp.where(allowed, scores, -1e30)
        peak = jnp.max(scores, axis=-1, keepdims=True)
        weights = jnp.where(allowed, jnp.exp(scores - peak), 0.0)
        totals = jnp.sum(weights, axis=-1, keepdims=True)
        totals = jnp.where(row_image < IMG, totals, 1.0)
        share = weights / totals
        shares[i] = share
        mixed = dot(share.astype(BF16), qkv[2, start : start + 2 * CAP, :])
        att[i * CAP : (i + 1) * CAP, :] = one_head(mixed).astype(BF16)

    attx[...] = dot(move[...], att[...], 0, 0).astype(BF16)
    pa[c, z] = attx[ROWS:, :]
    za[0]()

    for k in (1, 7, 2, 6, 3, 5, 4):
        ref = gf.at[yat(-k), pl.ds(ROWS, CAP)]
        copy_to(ref, ref, img_s.at[k], img_r.at[k], tensor=yat(k)).wait_recv()
    cotangent = jnp.concatenate([gf[n] for n in range(NT)], axis=1)
    ga[...] = dot(move[...], dot(cotangent, wo[...], 1, 1).astype(BF16)).astype(BF16)

    gacc[...] = jnp.zeros(gacc.shape, F32)
    for i, start in enumerate(WINDOWS):
        window = slice(start, start + 2 * CAP)
        rows = slice(i * CAP, (i + 1) * CAP)
        share = shares[i]
        pull = two_heads(ga[rows, :])
        query = two_heads(qkv[0, rows, :])
        grad_share = dot(pull, qkv[2, window, :], 1, 1)
        inner = jnp.sum(share * grad_share, axis=-1, keepdims=True)
        grad_score = (0.125 * share * (grad_share - inner)).astype(BF16)
        gcat[rows, 0:NARROW] = one_head(dot(grad_score, qkv[1, window, :])).astype(BF16)
        gacc[0, window, :] += dot(grad_score, query, 0, 0)
        gacc[1, window, :] += dot(share.astype(BF16), pull, 0, 0)
    gcat[:, NARROW : 2 * NARROW] = gacc[0].astype(BF16)
    gcat[:, 2 * NARROW :] = gacc[1].astype(BF16)

    mine = (3 - c, c)
    other = (2 + c, 1 - c)

    def core_msg(s):
        return copy_to(part.at[other[s]], crecv.at[s], core_s.at[s], core_r.at[s], dp=sibling)

    for n in range(NT):
        part[3, n * NARROW : (n + 1) * NARROW, :] = dot(attx[...], gf[n], 0, 0).astype(BF16)
    for n in range(NT):
        grads = dot(tf[n], gcat[...], 0, 0)
        for j in range(3):
            part[j, n * NARROW : (n + 1) * NARROW, :] = grads[
                :, j * NARROW : (j + 1) * NARROW
            ].astype(BF16)
    go(core_msg(0))
    go(core_msg(1))

    for n in range(NT):
        weight = jnp.concatenate([wi[j, n * NARROW : (n + 1) * NARROW, :] for j in range(3)], axis=1)
        pback[n] = dot(gcat[...], weight, 1, 1).astype(BF16)

    def reduce_y(buf, land, which):
        def piece(step, way, half):
            return (
                buf.at[yat(way * (5 - step)), pl.ds(half * HALF, HALF)],
                land.at[step - 1, (way + 1) // 2, pl.ds(half * HALF, HALF)],
                which * 16 + ((step - 1) * 2 + (way + 1) // 2) * 2 + half,
            )

        def msg(step, way, half):
            src, dst, sem = piece(step, way, half)
            return copy_to(src, dst, rs_s.at[sem], rs_r.at[sem], tensor=yat(way))

        def begin():
            for way in (1, -1):
                go(msg(1, way, (1 - way) // 2))

        def move(step):
            for half in range(2):
                for way in (1, -1):
                    if step > 2 or half == (1 - way) // 2:
                        msg(step - 1, way, half).wait_recv()
                        src, _, _ = piece(step, way, half)
                        _, got, _ = piece(step - 1, way, half)
                        src[...] = (src[...].astype(F32) + got[...].astype(F32)).astype(BF16)
                    go(msg(step, way, half))

        def finish(out):
            for half in range(2):
                for way in (1, -1):
                    msg(4, way, half).wait_recv()
            out[...] = (
                buf[t].astype(F32) + land[3, 0].astype(F32) + land[3, 1].astype(F32)
            ).astype(BF16)

        return begin, move, finish

    back = reduce_y(pback, rback, 0)
    outs = reduce_y(pout, rout, 1)
    back[0]()

    def core_sum(s):
        core_msg(s).wait_recv()
        csum[s] = (part[mine[s]].astype(F32) + crecv[s].astype(F32)).astype(BF16)

    def xr_msg(s, k):
        peer = xat(k)
        return copy_to(
            csum.at[s, pl.ds(pl.multiple_of(peer * 256, 256), 256)],
            xrecv.at[s, k - 1],
            xr_s.at[s, k],
            xr_r.at[s, k],
            outer=peer,
        )

    def x_send(s):
        for k in (2, 1, 3):
            go(xr_msg(s, k))

    def x_sum(s):
        for k in (1, 3, 2):
            xr_msg(s, k).wait_recv()
        acc = csum[s, pl.ds(pl.multiple_of(o * 256, 256), 256), :].astype(F32)
        for k in range(3):
            acc = acc + xrecv[s, k].astype(F32)
        tsum[s] = acc.astype(BF16)

    def far_first(m):
        half = lax.div(m + 1, 2)
        return 8 + half * (1 - 2 * lax.rem(m, 2))

    def zr_msg(s, k):
        peer = lax.rem(z + k, NZ)
        return copy_to(
            tsum.at[s, pl.ds(pl.multiple_of(peer * 16, 16), 16)],
            zrecv.at[s, k],
            zr_s.at[s, k],
            zr_r.at[s, k],
            dp=2 * peer + c,
        )

    def z_rows(place_z):
        return pl.ds(pl.multiple_of(o * 256 + place_z * 16, 16), 16)

    def zb_msg(s, k):
        peer = lax.rem(z + k, NZ)
        ref = full.at[mine[s], z_rows(z)]
        return copy_to(ref, ref, zb_s.at[s, k], zb_r.at[s, k], dp=2 * peer + c)

    def each_z(fn):
        def body(m, carry):
            fn(far_first(m))
            return carry

        lax.fori_loop(0, NZ - 1, body, 0)

    def z_send(s):
        each_z(lambda k: zr_msg(s, k).start())

    def z_sum(s):
        each_z(lambda k: zr_msg(s, k).wait_recv())
        acc = tsum[s, pl.ds(pl.multiple_of(z * 16, 16), 16), :].astype(F32)
        for k in range(1, NZ):
            acc = acc + zrecv[s, k].astype(F32)
        full[mine[s], z_rows(z), :] = acc.astype(BF16)
        each_z(lambda k: zb_msg(s, k).start())

    def xb_msg(s, k):
        ref = full.at[mine[s], pl.ds(pl.multiple_of(o * 256, 256), 256)]
        return copy_to(ref, ref, xb_s.at[s, k], xb_r.at[s, k], outer=xat(k))

    def xb_wait(s, k):
        ref = full.at[mine[s], pl.ds(pl.multiple_of(xat(NX - k) * 256, 256), 256)]
        copy_to(ref, ref, xb_s.at[s, k], xb_r.at[s, k], outer=xat(k)).wait_recv()

    def cb_msg(s, k):
        ref = full.at[mine[s], pl.ds(pl.multiple_of(xat(NX - k) * 256, 256), 256)]
        return copy_to(ref, ref, cb_s.at[s, k], cb_r.at[s, k], dp=sibling)

    def cb_wait(s, k):
        ref = full.at[other[s], pl.ds(pl.multiple_of(xat(NX - k) * 256, 256), 256)]
        copy_to(ref, ref, cb_s.at[s, k], cb_r.at[s, k], dp=sibling).wait_recv()

    def z_got(s, k):
        ref = full.at[mine[s], z_rows(lax.rem(z + (NZ - k), NZ))]
        peer = lax.rem(z + k, NZ)
        copy_to(ref, ref, zb_s.at[s, k], zb_r.at[s, k], dp=2 * peer + c).wait_recv()

    def spread_x(s):
        each_z(lambda k: z_got(s, k))
        for k in (2, 1, 3):
            go(xb_msg(s, k))
        go(cb_msg(s, 0))

    def spread_core(s):
        for k in (1, 3, 2):
            xb_wait(s, k)
            go(cb_msg(s, k))

    za[1]()
    core_sum(0)
    x_send(0)
    core_sum(1)
    x_send(1)
    za[2]()
    back[1](2)
    za[3]()
    x_sum(0)
    z_send(0)
    x_sum(1)
    z_send(1)
    za[4]()

    coming = one_if(dest_all == here) * one_if(lane3 != group)
    coming = coming * one_if(lane3 >= group - here) * one_if(lane3 < group - here + NDP)
    in_len = jnp.sum(jnp.sum(coming * blocks_all, axis=1, keepdims=True), axis=0, keepdims=True)
    source = jnp.sum(
        jnp.sum(coming * (lane3 - group + here), axis=1, keepdims=True), axis=0, keepdims=True
    )
    put_row, put_col = count((ROWS, CAP), 0), count((ROWS, CAP), 1)
    put = one_if(put_row == put_col + BLOCK * kept_total) * one_if(put_col < BLOCK * in_len)
    incoming = dot(put.astype(BF16), pick(pa, source))
    att[...] = (attx[:ROWS, :].astype(F32) + incoming).astype(BF16)
    for n in range(NT):
        pout[n] = dot(att[...], wo[:, n * NARROW : (n + 1) * NARROW]).astype(BF16)
    outs[0]()
    back[1](3)
    outs[1](2)
    back[1](4)
    z_sum(0)
    z_sum(1)
    outs[1](3)
    back[2](gtok_o)
    outs[1](4)
    spread_x(0)
    spread_x(1)
    outs[2](lay_o)
    spread_core(0)
    spread_core(1)
    for s in range(2):
        for k in (0, 1, 3, 2):
            cb_wait(s, k)
    giw_o[...] = full[0:3]
    for n in range(NT):
        gow_o[:, n * NARROW : (n + 1) * NARROW] = full[3, n * NARROW : (n + 1) * NARROW, :]

    for cp in pending:
        cp.wait_send()
    for s in range(2):
        each_z(lambda k: zr_msg(s, k).wait_send())
        each_z(lambda k: zb_msg(s, k).wait_send())


def on_device(tokens, input_weight, output_weight, grad_layer, patch_blocks, target_group):
    vmem = pl.BlockSpec(memory_space=pltpu.VMEM)
    dma = pltpu.SemaphoreType.DMA

    def buf(*shape, dtype=BF16):
        return pltpu.VMEM(shape, dtype)

    layer_out, grad_tokens, input_sum, output_sum = pl.pallas_call(
        kernel,
        out_shape=(
            jax.ShapeDtypeStruct((ROWS, NARROW), BF16),
            jax.ShapeDtypeStruct((ROWS, NARROW), BF16),
            jax.ShapeDtypeStruct((3, NT * NARROW, NARROW), BF16),
            jax.ShapeDtypeStruct((NARROW, NT * NARROW), BF16),
        ),
        in_specs=[vmem] * 6,
        out_specs=(vmem,) * 4,
        scratch_shapes=[
            buf(NT, ROWS, NARROW),
            buf(NT, EXTRA, NARROW),
            buf(2, NZ, CAP, NARROW),
            buf(2, NZ, CAP, NARROW),
            buf(ROWS, EXTRA),
            buf(3, ROWS, NARROW),
            buf(ROWS, NARROW),
            buf(3, 2 * CAP, 2 * CAP, dtype=F32),
            buf(ROWS, NARROW),
            buf(EXTRA, NARROW),
            buf(ROWS, 3 * NARROW),
            buf(2, ROWS, NARROW, dtype=F32),
            buf(4, 1024, NARROW),
            buf(2, 1024, NARROW),
            buf(2, 1024, NARROW),
            buf(2, 3, 256, NARROW),
            buf(2, 256, NARROW),
            buf(2, NZ, 16, NARROW),
            buf(4, 1024, NARROW),
            buf(NT, ROWS, NARROW),
            buf(NT, ROWS, NARROW),
            buf(4, 2, ROWS, NARROW),
            buf(4, 2, ROWS, NARROW),
            dma((32,)), dma((32,)),
            dma((NT,)), dma((NT,)),
            dma((NZ + 1,)), dma((NZ + 1,)),
            dma((NZ + 1,)), dma((NZ + 1,)),
            dma((2,)), dma((2,)),
            dma((2,)), dma((2,)),
            dma((2, NX)), dma((2, NX)),
            dma((2, NZ)), dma((2, NZ)),
            dma((2, NZ)), dma((2, NZ)),
            dma((2, NX)), dma((2, NX)),
            dma((2, NX)), dma((2, NX)),
            dma((32,)), dma((32,)),
        ],
        compiler_params=pltpu.CompilerParams(
            collective_id=0, has_side_effects=True, vmem_limit_bytes=56 * 2**20
        ),
    )(
        tokens,
        jnp.transpose(input_weight, (1, 0, 2)),
        output_weight,
        grad_layer,
        patch_blocks.T,
        target_group.T,
    )
    grad_input_weight = jnp.transpose(input_sum, (1, 0, 2)).astype(F32)
    return layer_out, grad_tokens, grad_input_weight, output_sum.astype(F32)


def solution(mesh):
    return jax.shard_map(
        on_device,
        mesh=mesh,
        in_specs=(
            P(("outer", "dp"), "tensor"),
            P(None, None, "tensor"),
            P("tensor", None),
            P(("outer", "dp"), "tensor"),
            P(),
            P(),
        ),
        out_specs=(
            P(("outer", "dp"), "tensor"),
            P(("outer", "dp"), "tensor"),
            P(None, None, "tensor"),
            P("tensor", None),
        ),
        check_vma=False,
    )
```

```python
import jax
import jax.numpy as jnp
from jax import lax
from jax.experimental import pallas as pl
from jax.experimental.pallas import tpu as pltpu
from jax.sharding import PartitionSpec as P

MESH = pl.DeviceIdType.MESH
BF16 = jnp.bfloat16
F32 = jnp.float32

ROWS = 384
NARROW = 128
BLOCK = 64
BLOCKS = 6
IMG = 3
CAP = 128
NT = 8
NZ = 16
NX = 4
NDP = 32
NEAR = 4
HALF = ROWS // 2
EXTRA = ROWS + CAP
WINDOWS = (0, 64, 128)


def dot(a, b, ca=1, cb=0):
    return lax.dot_general(a, b, (((ca,), (cb,)), ((), ())), preferred_element_type=F32)


def one_if(condition):
    return jnp.where(condition, 1.0, 0.0)


def count(shape, axis):
    return lax.broadcasted_iota(jnp.int32, shape, axis).astype(F32)


def copy_to(src, dst, send, recv, **device):
    return pltpu.make_async_remote_copy(
        src_ref=src,
        dst_ref=dst,
        send_sem=send,
        recv_sem=recv,
        device_id=device,
        device_id_type=MESH,
    )


def kernel(
    tok, wi_hbm, wo_hbm, gl, pb, tg,
    lay_o, gtok_o, sum_o,
    wi, wo, tf, tft, gf, pg, pa, give, got, move, qkv, ga, gax, shares, att, attx, gcat, gacc, gowacc,
    lay, gtok, part, csum, crecv, xrecv, tsum, zrecv, full,
    pback, pout, rback, rout,
    ring_s, ring_r, img_s, img_r, zg_s, zg_r, za_s, za_r, sib_s, sib_r,
    load, store, core_s, core_r, xr_s, xr_r, zr_s, zr_r, zb_s, zb_r, xb_s, xb_r, cb_s, cb_r,
    rs_s, rs_r,
):
    o = lax.axis_index("outer")
    d = lax.axis_index("dp")
    t = lax.axis_index("tensor")
    z = lax.div(d, 2)
    c = lax.rem(d, 2)
    sibling = d + 1 - 2 * c

    def yat(k):
        return lax.rem(t + (k + NT), NT)

    def zat(k):
        return lax.rem(z + (k + NZ), NZ)

    def xat(k):
        return lax.rem(o + k, NX)

    pending = []

    def go(cp):
        cp.start()
        pending.append(cp)

    loads = [
        pltpu.make_async_copy(gl, gf.at[t, pl.ds(0, ROWS)], load.at[0]),
        pltpu.make_async_copy(tok, tf.at[t], load.at[1]),
        pltpu.make_async_copy(wi_hbm, wi, load.at[2]),
        pltpu.make_async_copy(wo_hbm, wo, load.at[3]),
    ]
    for cp in loads:
        cp.start()

    barrier = pltpu.get_barrier_semaphore()

    def greet(**device):
        pl.semaphore_signal(barrier, inc=1, device_id=device, device_id_type=MESH)

    for k in range(1, NEAR + 1):
        greet(dp=2 * zat(k) + c)
        greet(dp=2 * zat(-k) + c)
    greet(dp=sibling)
    for k in range(1, NT):
        greet(tensor=yat(k))
    for k in range(1, NX):
        greet(outer=xat(k))

    here = d.astype(F32)
    beside = sibling.astype(F32)
    lane3 = count((IMG, NARROW), 1)
    blocks_all = pb[...].astype(F32)
    dest_all = tg[...].astype(F32)

    def own_of(table, owner):
        mark = one_if(lane3 == (o * NDP).astype(F32) + owner)
        return jnp.sum(table * mark, axis=1, keepdims=True)

    def target_of(owner):
        takers = own_of(dest_all, owner)
        return jnp.sum(takers * one_if(takers != owner), axis=0, keepdims=True)

    def coming_to(owner):
        base = (o * NDP).astype(F32)
        mark = one_if(dest_all == owner) * one_if(lane3 != base + owner)
        return mark * one_if(lane3 >= base) * one_if(lane3 < base + NDP)

    def source_of(owner):
        marks = coming_to(owner) * (lane3 - (o * NDP).astype(F32))
        return jnp.sum(jnp.sum(marks, axis=1, keepdims=True), axis=0, keepdims=True)

    length3 = own_of(blocks_all, here)
    dest3 = own_of(dest_all, here)
    length = [length3[i : i + 1] for i in range(IMG)]
    dest = [dest3[i : i + 1] for i in range(IMG)]
    first = [jnp.zeros((1, 1), F32), length[0], length[0] + length[1]]
    total = first[2] + length[2]
    stays = [one_if(dest[i] == here) for i in range(IMG)]
    moved = [1.0 - stays[i] for i in range(IMG)]
    kept = [stays[i] * length[i] for i in range(IMG)]
    place = [jnp.zeros((1, 1), F32), kept[0], kept[0] + kept[1]]
    kept_total = place[2] + kept[2]

    cut = one_if(count((CAP, ROWS), 1) == count((CAP, ROWS), 0) + BLOCK * kept_total)
    cut = cut.astype(BF16)
    loads[0].wait()
    pg[z] = dot(cut, gf[t, :ROWS, :]).astype(BF16)
    loads[1].wait()

    pl.semaphore_wait(barrier, 2 * NEAR + 1 + (NT - 1) + (NX - 1))

    def gather_z(buf, ss, rs, n):
        def msg(a, j, half=None):
            k = (a + j) % NZ
            sem = NZ if half == 1 else k
            ref = buf.at[zat(-a)]
            if half is not None:
                ref = ref.at[pl.ds(half * BLOCK, BLOCK)]
            return copy_to(ref, ref, ss.at[sem], rs.at[sem], dp=2 * zat(j) + c)

        def arrived(k, half=None):
            sem = NZ if half == 1 else k
            ref = buf.at[zat(-k)]
            if half is not None:
                ref = ref.at[pl.ds(half * BLOCK, BLOCK)]
            copy_to(ref, ref, ss.at[sem], rs.at[sem], dp=2 * zat(k) + c).wait_recv()

        def one():
            for j in (4, -4, 2, -2, 1, -1):
                go(msg(0, j))

        def two():
            arrived(4)
            go(msg(4, 4, 0))
            arrived(12)
            go(msg(-4, -4, 1))
            for j in (3, 2, 1, -1):
                go(msg(4, j))
                go(msg(-4, -j))

        def cross():
            return copy_to(give.at[n], got.at[n], sib_s.at[n], sib_r.at[n], dp=sibling)

        def pick(peer):
            acc = jnp.zeros((CAP, NARROW), BF16)
            for k in range(NZ):
                mark = one_if(peer == (c + 2 * k).astype(F32))
                acc = acc + buf[k] * jnp.broadcast_to(mark, (1, NARROW)).astype(BF16)
            return acc

        def three(other_peer):
            for k in (1, 15, 2, 14, 3, 13, 5, 11, 6, 10, 7, 9):
                arrived(k)
            arrived(8, 0)
            arrived(8, 1)
            give[n] = pick(other_peer)
            go(cross())

        def four(peer):
            acc = pick(peer)
            cross().wait_recv()
            return acc + got[n]

        return one, two, three, four

    zg = gather_z(pg, zg_s, zg_r, 0)
    za = gather_z(pa, za_s, za_r, 1)

    def ring_msg(step, way, buf, n, half):
        slot = yat(-way * (step - 1))
        ref = buf.at[slot, pl.ds(half * HALF, HALF)]
        sem = ((step - 1) * 2 + (way + 1) // 2) * 4 + n * 2 + half
        return copy_to(ref, ref, ring_s.at[sem], ring_r.at[sem], tensor=yat(way))

    def ring_sends(step):
        for half in range(2):
            for n, buf in enumerate((tf, gf)):
                for way in (1, -1):
                    if step < 4 or half == (1 - way) // 2:
                        go(ring_msg(step, way, buf, n, half))

    def ring_waits(step):
        for half in range(2):
            for n, buf in enumerate((tf, gf)):
                for way in (1, -1):
                    if step < 4 or half == (1 - way) // 2:
                        slot = yat(-way * step)
                        ref = buf.at[slot, pl.ds(half * HALF, HALF)]
                        sem = ((step - 1) * 2 + (way + 1) // 2) * 4 + n * 2 + half
                        copy_to(
                            ref, ref, ring_s.at[sem], ring_r.at[sem], tensor=yat(way)
                        ).wait_recv()
                        if step < 3 or (step == 3 and half == (1 - way) // 2):
                            go(ring_msg(step + 1, way, buf, n, half))

    zg[0]()
    ring_sends(1)
    zg[1]()
    ring_waits(1)
    ring_waits(2)
    zg[2](target_of(beside))

    gf[t, ROWS:, :] = zg[3](target_of(here))
    img_ref = gf.at[t, pl.ds(ROWS, CAP)]
    for k in (4, 3, 5, 2, 6, 1, 7):
        go(copy_to(img_ref, img_ref, img_s.at[k], img_r.at[k], tensor=yat(k)))
    ring_waits(3)
    ring_waits(4)

    loads[2].wait()
    loads[3].wait()
    tokens = jnp.concatenate([tf[n] for n in range(NT)], axis=1)
    for j in range(3):
        qkv[j] = dot(tokens, wi[j]).astype(BF16)

    lane = lax.broadcasted_iota(jnp.int32, (1, NARROW), 1)
    low = lane < BLOCK
    zero = jnp.zeros((), F32)

    def two_heads(x):
        x = x.astype(F32)
        return jnp.concatenate(
            [jnp.where(low, x, zero).astype(BF16), jnp.where(low, zero, x).astype(BF16)], axis=0
        )

    def one_head(x):
        return jnp.where(low, x[:CAP], x[CAP:])

    row = count((ROWS, 1), 0)
    column = jnp.full((ROWS, 1), -1.0, F32)
    for i in range(IMG):
        inside = one_if(row >= BLOCK * first[i]) * one_if(row < BLOCK * (first[i] + length[i]))
        shift = BLOCK * (stays[i] * place[i] + moved[i] * BLOCKS - first[i])
        column = column + inside * (row + shift + 1.0)
    move[...] = one_if(count((ROWS, EXTRA), 1) == column).astype(BF16)

    def image_of(position):
        marks = jnp.zeros(position.shape, F32)
        for edge in (first[1], first[2], total):
            marks = marks + one_if(position >= edge * BLOCK)
        return marks

    for i, start in enumerate(WINDOWS):
        place_in = count((2 * CAP, 1), 0)
        row_image = image_of(place_in - CAP * one_if(place_in >= CAP) + i * CAP)
        key_image = image_of(count((1, 2 * CAP), 1) + start)
        allowed = (row_image == key_image) & (row_image < IMG)
        query = two_heads(qkv[0, i * CAP : (i + 1) * CAP, :])
        scores = dot(query, qkv[1, start : start + 2 * CAP, :], 1, 1) * 0.125
        scores = jnp.where(allowed, scores, -1e30)
        peak = jnp.max(scores, axis=-1, keepdims=True)
        weights = jnp.where(allowed, jnp.exp(scores - peak), 0.0)
        totals = jnp.sum(weights, axis=-1, keepdims=True)
        totals = jnp.where(row_image < IMG, totals, 1.0)
        share = weights / totals
        shares[i] = share
        mixed = dot(share.astype(BF16), qkv[2, start : start + 2 * CAP, :])
        att[i * CAP : (i + 1) * CAP, :] = one_head(mixed).astype(BF16)

    attx[...] = dot(move[...], att[...], 0, 0).astype(BF16)
    pa[z] = attx[ROWS:, :]
    za[0]()

    for n in range(NT):
        tft[n] = tf[n].T
    cotangent = jnp.concatenate([gf[n, :ROWS, :] for n in range(NT)], axis=1)
    gax[:ROWS, :] = dot(cotangent, wo[...], 1, 1).astype(BF16)
    for n in range(NT):
        gowacc[n] = dot(attx[:ROWS, :], gf[n, :ROWS, :], 0, 0)

    for k in (1, 7, 2, 6, 3, 5, 4):
        ref = gf.at[yat(-k), pl.ds(ROWS, CAP)]
        copy_to(ref, ref, img_s.at[k], img_r.at[k], tensor=yat(k)).wait_recv()
    cotangent = jnp.concatenate([gf[n, ROWS:, :] for n in range(NT)], axis=1)
    gax[ROWS:, :] = dot(cotangent, wo[...], 1, 1).astype(BF16)
    ga[...] = dot(move[...], gax[...]).astype(BF16)

    gacc[...] = jnp.zeros(gacc.shape, F32)
    for i, start in enumerate(WINDOWS):
        window = slice(start, start + 2 * CAP)
        rows = slice(i * CAP, (i + 1) * CAP)
        share = shares[i]
        pull = two_heads(ga[rows, :])
        query = two_heads(qkv[0, rows, :])
        grad_share = dot(pull, qkv[2, window, :], 1, 1)
        inner = jnp.sum(share * grad_share, axis=-1, keepdims=True)
        grad_score = (0.125 * share * (grad_share - inner)).astype(BF16)
        gcat[rows, 0:NARROW] = one_head(dot(grad_score, qkv[1, window, :])).astype(BF16)
        gacc[0, window, :] += dot(grad_score, query, 0, 0)
        gacc[1, window, :] += dot(share.astype(BF16), pull, 0, 0)
    gcat[:, NARROW : 2 * NARROW] = gacc[0].astype(BF16)
    gcat[:, 2 * NARROW :] = gacc[1].astype(BF16)

    mine = (3 - c, c)
    other = (2 + c, 1 - c)

    def core_msg(s):
        return copy_to(part.at[other[s]], crecv.at[s], core_s.at[s], core_r.at[s], dp=sibling)

    for n in range(NT):
        rows = slice(n * NARROW, (n + 1) * NARROW)
        part[2, rows, :] = dot(tft[n], gcat[:, 2 * NARROW :]).astype(BF16)
        part[3, rows, :] = (gowacc[n] + dot(attx[ROWS:, :], gf[n, ROWS:, :], 0, 0)).astype(BF16)
    go(core_msg(0))
    for n in range(NT):
        rows = slice(n * NARROW, (n + 1) * NARROW)
        grads = dot(tft[n], gcat[:, : 2 * NARROW])
        part[0, rows, :] = grads[:, :NARROW].astype(BF16)
        part[1, rows, :] = grads[:, NARROW:].astype(BF16)
    go(core_msg(1))

    def reduce_y(buf, land, which):
        def piece(step, way, half):
            return (
                buf.at[yat(way * (5 - step)), pl.ds(half * HALF, HALF)],
                land.at[step - 1, (way + 1) // 2, pl.ds(half * HALF, HALF)],
                which * 16 + ((step - 1) * 2 + (way + 1) // 2) * 2 + half,
            )

        def msg(step, way, half):
            src, dst, sem = piece(step, way, half)
            return copy_to(src, dst, rs_s.at[sem], rs_r.at[sem], tensor=yat(way))

        def begin():
            for way in (1, -1):
                go(msg(1, way, (1 - way) // 2))

        def move(step):
            for half in range(2):
                for way in (1, -1):
                    if step > 2 or half == (1 - way) // 2:
                        msg(step - 1, way, half).wait_recv()
                        src, _, _ = piece(step, way, half)
                        _, got, _ = piece(step - 1, way, half)
                        src[...] = (src[...].astype(F32) + got[...].astype(F32)).astype(BF16)
                    go(msg(step, way, half))

        def finish(out):
            for half in range(2):
                for way in (1, -1):
                    msg(4, way, half).wait_recv()
            out[...] = (
                buf[t].astype(F32) + land[3, 0].astype(F32) + land[3, 1].astype(F32)
            ).astype(BF16)

        return begin, move, finish

    back = reduce_y(pback, rback, 0)
    outs = reduce_y(pout, rout, 1)

    def core_sum(s):
        core_msg(s).wait_recv()
        csum[s] = (part[mine[s]].astype(F32) + crecv[s].astype(F32)).astype(BF16)

    def xr_msg(s, k):
        peer = xat(k)
        return copy_to(
            csum.at[s, pl.ds(pl.multiple_of(peer * 256, 256), 256)],
            xrecv.at[s, k - 1],
            xr_s.at[s, k],
            xr_r.at[s, k],
            outer=peer,
        )

    def x_send(s):
        for k in (2, 1, 3):
            go(xr_msg(s, k))

    def x_sum(s):
        for k in (1, 3, 2):
            xr_msg(s, k).wait_recv()
        acc = csum[s, pl.ds(pl.multiple_of(o * 256, 256), 256), :].astype(F32)
        for k in range(3):
            acc = acc + xrecv[s, k].astype(F32)
        tsum[s] = acc.astype(BF16)

    def far_first(m):
        half = lax.div(m + 1, 2)
        return 8 + half * (1 - 2 * lax.rem(m, 2))

    def zr_msg(s, k):
        peer = lax.rem(z + k, NZ)
        return copy_to(
            tsum.at[s, pl.ds(pl.multiple_of(peer * 16, 16), 16)],
            zrecv.at[s, k],
            zr_s.at[s, k],
            zr_r.at[s, k],
            dp=2 * peer + c,
        )

    def z_rows(place_z):
        return pl.ds(pl.multiple_of(o * 256 + place_z * 16, 16), 16)

    def zb_msg(s, k):
        peer = lax.rem(z + k, NZ)
        ref = full.at[mine[s], z_rows(z)]
        return copy_to(ref, ref, zb_s.at[s, k], zb_r.at[s, k], dp=2 * peer + c)

    def each_z(fn):
        def body(m, carry):
            fn(far_first(m))
            return carry

        lax.fori_loop(0, NZ - 1, body, 0)

    def z_send(s):
        each_z(lambda k: zr_msg(s, k).start())

    def z_sum(s):
        each_z(lambda k: zr_msg(s, k).wait_recv())
        acc = tsum[s, pl.ds(pl.multiple_of(z * 16, 16), 16), :].astype(F32)
        for k in range(1, NZ):
            acc = acc + zrecv[s, k].astype(F32)
        full[mine[s], z_rows(z), :] = acc.astype(BF16)
        each_z(lambda k: zb_msg(s, k).start())

    def xb_msg(s, k):
        ref = full.at[mine[s], pl.ds(pl.multiple_of(o * 256, 256), 256)]
        return copy_to(ref, ref, xb_s.at[s, k], xb_r.at[s, k], outer=xat(k))

    def xb_wait(s, k):
        ref = full.at[mine[s], pl.ds(pl.multiple_of(xat(NX - k) * 256, 256), 256)]
        copy_to(ref, ref, xb_s.at[s, k], xb_r.at[s, k], outer=xat(k)).wait_recv()

    def cb_msg(s, k):
        ref = full.at[mine[s], pl.ds(pl.multiple_of(xat(NX - k) * 256, 256), 256)]
        return copy_to(ref, ref, cb_s.at[s, k], cb_r.at[s, k], dp=sibling)

    def cb_wait(s, k):
        ref = full.at[other[s], pl.ds(pl.multiple_of(xat(NX - k) * 256, 256), 256)]
        copy_to(ref, ref, cb_s.at[s, k], cb_r.at[s, k], dp=sibling).wait_recv()

    def z_got(s, k):
        ref = full.at[mine[s], z_rows(lax.rem(z + (NZ - k), NZ))]
        peer = lax.rem(z + k, NZ)
        copy_to(ref, ref, zb_s.at[s, k], zb_r.at[s, k], dp=2 * peer + c).wait_recv()

    def spread_x(s):
        each_z(lambda k: z_got(s, k))
        for k in (2, 1, 3):
            go(xb_msg(s, k))
        go(cb_msg(s, 0))

    def spread_core(s):
        for k in (1, 3, 2):
            xb_wait(s, k)
            go(cb_msg(s, k))

    core_sum(0)
    x_send(0)
    core_sum(1)
    x_send(1)
    za[1]()

    for n in range(NT):
        weight = jnp.concatenate([wi[j, n * NARROW : (n + 1) * NARROW, :] for j in range(3)], axis=1)
        pback[n] = dot(gcat[...], weight, 1, 1).astype(BF16)
    back[0]()
    x_sum(0)
    z_send(0)
    x_sum(1)
    z_send(1)
    za[2](source_of(beside))
    back[1](2)

    in_len = jnp.sum(
        jnp.sum(coming_to(here) * blocks_all, axis=1, keepdims=True), axis=0, keepdims=True
    )
    put_row, put_col = count((ROWS, CAP), 0), count((ROWS, CAP), 1)
    put = one_if(put_row == put_col + BLOCK * kept_total) * one_if(put_col < BLOCK * in_len)
    incoming = dot(put.astype(BF16), za[3](source_of(here)))
    att[...] = (attx[:ROWS, :].astype(F32) + incoming).astype(BF16)
    for n in range(NT):
        pout[n] = dot(att[...], wo[:, n * NARROW : (n + 1) * NARROW]).astype(BF16)
    outs[0]()
    back[1](3)
    z_sum(0)
    z_sum(1)
    outs[1](2)
    back[1](4)
    outs[1](3)
    stores = []

    def keep(src, dst):
        cp = pltpu.make_async_copy(src, dst, store.at[len(stores)])
        cp.start()
        stores.append(cp)

    def keep_piece(chunk, k):
        rows = pl.ds(pl.multiple_of(xat(NX - k) * 256, 256), 256)
        keep(full.at[chunk, rows], sum_o.at[chunk, rows])

    back[2](gtok)
    keep(gtok, gtok_o)
    spread_x(0)
    spread_x(1)
    outs[1](4)
    for s in range(2):
        spread_core(s)
        for k in range(NX):
            keep_piece(mine[s], k)
    outs[2](lay)
    keep(lay, lay_o)
    for s in range(2):
        for k in (0, 1, 3, 2):
            cb_wait(s, k)
            keep_piece(other[s], k)

    for cp in pending:
        cp.wait_send()
    for s in range(2):
        each_z(lambda k: zr_msg(s, k).wait_send())
        each_z(lambda k: zb_msg(s, k).wait_send())
    for cp in stores:
        cp.wait()


def finish(
    lay_i, gtok_i, sum_i, lay_o, gtok_o, giw_o, gow_o, low, wide, flat, lay, gtok, sem_i, sem_o
):
    reads = [pltpu.make_async_copy(sum_i.at[j], low.at[j], sem_i.at[j]) for j in range(4)]
    reads.append(pltpu.make_async_copy(lay_i, lay, sem_i.at[4]))
    reads.append(pltpu.make_async_copy(gtok_i, gtok, sem_i.at[5]))
    copies = []
    for cp in reads:
        cp.start()
    for j in range(3):
        reads[j].wait()
        wide[j] = low[j].astype(F32)
        copies.append(pltpu.make_async_copy(wide.at[j], giw_o.at[j], sem_o.at[j]))
        copies[-1].start()
    reads[3].wait()
    for n in range(NT):
        columns = slice(n * NARROW, (n + 1) * NARROW)
        flat[:, columns] = low[3, columns, :].astype(F32)
    copies.append(pltpu.make_async_copy(flat, gow_o, sem_o.at[3]))
    copies[-1].start()
    for j, src, dst in ((4, lay, lay_o), (5, gtok, gtok_o)):
        reads[j].wait()
        copies.append(pltpu.make_async_copy(src, dst, sem_o.at[j]))
        copies[-1].start()
    for cp in copies:
        cp.wait()


def on_device(tokens, input_weight, output_weight, grad_layer, patch_blocks, target_group):
    vmem = pl.BlockSpec(memory_space=pltpu.VMEM)
    hbm = pl.BlockSpec(memory_space=pl.ANY)
    dma = pltpu.SemaphoreType.DMA

    def buf(*shape, dtype=BF16):
        return pltpu.VMEM(shape, dtype)

    rows_bf16 = jax.ShapeDtypeStruct((ROWS, NARROW), BF16)
    layer_out, grad_tokens, sums = pl.pallas_call(
        kernel,
        out_shape=(rows_bf16, rows_bf16, jax.ShapeDtypeStruct((4, NT * NARROW, NARROW), BF16)),
        in_specs=[hbm] * 4 + [vmem] * 2,
        out_specs=(hbm,) * 3,
        scratch_shapes=[
            buf(3, 1024, NARROW),
            buf(NARROW, 1024),
            buf(NT, ROWS, NARROW),
            buf(NT, NARROW, ROWS),
            buf(NT, EXTRA, NARROW),
            buf(NZ, CAP, NARROW),
            buf(NZ, CAP, NARROW),
            buf(2, CAP, NARROW),
            buf(2, CAP, NARROW),
            buf(ROWS, EXTRA),
            buf(3, ROWS, NARROW),
            buf(ROWS, NARROW),
            buf(EXTRA, NARROW),
            buf(3, 2 * CAP, 2 * CAP, dtype=F32),
            buf(ROWS, NARROW),
            buf(EXTRA, NARROW),
            buf(ROWS, 3 * NARROW),
            buf(2, ROWS, NARROW, dtype=F32),
            buf(NT, NARROW, NARROW, dtype=F32),
            buf(ROWS, NARROW),
            buf(ROWS, NARROW),
            buf(4, 1024, NARROW),
            buf(2, 1024, NARROW),
            buf(2, 1024, NARROW),
            buf(2, 3, 256, NARROW),
            buf(2, 256, NARROW),
            buf(2, NZ, 16, NARROW),
            buf(4, 1024, NARROW),
            buf(NT, ROWS, NARROW),
            buf(NT, ROWS, NARROW),
            buf(4, 2, ROWS, NARROW),
            buf(4, 2, ROWS, NARROW),
            dma((32,)), dma((32,)),
            dma((NT,)), dma((NT,)),
            dma((NZ + 1,)), dma((NZ + 1,)),
            dma((NZ + 1,)), dma((NZ + 1,)),
            dma((2,)), dma((2,)),
            dma((4,)), dma((18,)),
            dma((2,)), dma((2,)),
            dma((2, NX)), dma((2, NX)),
            dma((2, NZ)), dma((2, NZ)),
            dma((2, NZ)), dma((2, NZ)),
            dma((2, NX)), dma((2, NX)),
            dma((2, NX)), dma((2, NX)),
            dma((32,)), dma((32,)),
        ],
        compiler_params=pltpu.CompilerParams(
            collective_id=0, has_side_effects=True, vmem_limit_bytes=56 * 2**20
        ),
    )(
        tokens,
        jnp.transpose(input_weight, (1, 0, 2)),
        output_weight,
        grad_layer,
        patch_blocks.T,
        target_group.T,
    )
    layer_out, grad_tokens, input_sum, output_sum = pl.pallas_call(
        finish,
        out_shape=(
            rows_bf16,
            rows_bf16,
            jax.ShapeDtypeStruct((3, NT * NARROW, NARROW), F32),
            jax.ShapeDtypeStruct((NARROW, NT * NARROW), F32),
        ),
        in_specs=[hbm] * 3,
        out_specs=(hbm,) * 4,
        scratch_shapes=[
            buf(4, NT * NARROW, NARROW),
            buf(3, NT * NARROW, NARROW, dtype=F32),
            buf(NARROW, NT * NARROW, dtype=F32),
            buf(ROWS, NARROW),
            buf(ROWS, NARROW),
            dma((6,)),
            dma((6,)),
        ],
        compiler_params=pltpu.CompilerParams(vmem_limit_bytes=56 * 2**20),
    )(layer_out, grad_tokens, sums)
    return layer_out, grad_tokens, jnp.transpose(input_sum, (1, 0, 2)), output_sum


def solution(mesh):
    return jax.shard_map(
        on_device,
        mesh=mesh,
        in_specs=(
            P(("outer", "dp"), "tensor"),
            P(None, None, "tensor"),
            P("tensor", None),
            P(("outer", "dp"), "tensor"),
            P(),
            P(),
        ),
        out_specs=(
            P(("outer", "dp"), "tensor"),
            P(("outer", "dp"), "tensor"),
            P(None, None, "tensor"),
            P("tensor", None),
        ),
        check_vma=False,
    )
```

```python
import jax
import jax.numpy as jnp
from jax import lax
from jax.experimental import pallas as pl
from jax.experimental.pallas import tpu as pltpu
from jax.sharding import PartitionSpec as P

MESH = pl.DeviceIdType.MESH
BF16 = jnp.bfloat16
F32 = jnp.float32

ROWS = 384
NARROW = 128
BLOCK = 64
BLOCKS = 6
IMG = 3
CAP = 128
NT = 8
NZ = 16
NX = 4
NDP = 32
NEAR = 4
HALF = ROWS // 2
EXTRA = ROWS + CAP
WINDOWS = (0, 64, 128)


def dot(a, b, ca=1, cb=0):
    return lax.dot_general(a, b, (((ca,), (cb,)), ((), ())), preferred_element_type=F32)


def one_if(condition):
    return jnp.where(condition, 1.0, 0.0)


def count(shape, axis):
    return lax.broadcasted_iota(jnp.int32, shape, axis).astype(F32)


def copy_to(src, dst, send, recv, **device):
    return pltpu.make_async_remote_copy(
        src_ref=src,
        dst_ref=dst,
        send_sem=send,
        recv_sem=recv,
        device_id=device,
        device_id_type=MESH,
    )


def kernel(
    tok, wi_hbm, wo_hbm, gl, pb, tg,
    lay_o, gtok_o, sum_o,
    wi, wo, tf, tft, gf, pg, pa, give, got, move, qkv, ga, gax, shares, att, attx, gcat, gacc, gowacc,
    lay, gtok, part, csum, crecv, xrecv, tsum, zrecv, full,
    pback, pout, rback, rout,
    ring_s, ring_r, img_s, img_r, zg_s, zg_r, za_s, za_r, sib_s, sib_r,
    load, store, core_s, core_r, xr_s, xr_r, zr_s, zr_r, zb_s, zb_r, xb_s, xb_r, cb_s, cb_r,
    rs_s, rs_r,
):
    o = lax.axis_index("outer")
    d = lax.axis_index("dp")
    t = lax.axis_index("tensor")
    z = lax.div(d, 2)
    c = lax.rem(d, 2)
    sibling = d + 1 - 2 * c

    def yat(k):
        return lax.rem(t + (k + NT), NT)

    def zat(k):
        return lax.rem(z + (k + NZ), NZ)

    def xat(k):
        return lax.rem(o + k, NX)

    pending = []

    def go(cp):
        cp.start()
        pending.append(cp)

    loads = [
        pltpu.make_async_copy(gl, gf.at[t, pl.ds(0, ROWS)], load.at[0]),
        pltpu.make_async_copy(tok, tf.at[t], load.at[1]),
        pltpu.make_async_copy(wi_hbm, wi, load.at[2]),
        pltpu.make_async_copy(wo_hbm, wo, load.at[3]),
    ]
    for cp in loads:
        cp.start()

    barrier = pltpu.get_barrier_semaphore()

    def greet(**device):
        pl.semaphore_signal(barrier, inc=1, device_id=device, device_id_type=MESH)

    for k in range(1, NEAR + 1):
        greet(dp=2 * zat(k) + c)
        greet(dp=2 * zat(-k) + c)
    greet(dp=sibling)
    for k in range(1, NT):
        greet(tensor=yat(k))
    for k in range(1, NX):
        greet(outer=xat(k))

    here = d.astype(F32)
    beside = sibling.astype(F32)
    lane3 = count((IMG, NARROW), 1)
    blocks_all = pb[...].astype(F32)
    dest_all = tg[...].astype(F32)

    def own_of(table, owner):
        mark = one_if(lane3 == (o * NDP).astype(F32) + owner)
        return jnp.sum(table * mark, axis=1, keepdims=True)

    def target_of(owner):
        takers = own_of(dest_all, owner)
        return jnp.sum(takers * one_if(takers != owner), axis=0, keepdims=True)

    def coming_to(owner):
        base = (o * NDP).astype(F32)
        mark = one_if(dest_all == owner) * one_if(lane3 != base + owner)
        return mark * one_if(lane3 >= base) * one_if(lane3 < base + NDP)

    def source_of(owner):
        marks = coming_to(owner) * (lane3 - (o * NDP).astype(F32))
        return jnp.sum(jnp.sum(marks, axis=1, keepdims=True), axis=0, keepdims=True)

    length3 = own_of(blocks_all, here)
    dest3 = own_of(dest_all, here)
    length = [length3[i : i + 1] for i in range(IMG)]
    dest = [dest3[i : i + 1] for i in range(IMG)]
    first = [jnp.zeros((1, 1), F32), length[0], length[0] + length[1]]
    total = first[2] + length[2]
    stays = [one_if(dest[i] == here) for i in range(IMG)]
    moved = [1.0 - stays[i] for i in range(IMG)]
    kept = [stays[i] * length[i] for i in range(IMG)]
    place = [jnp.zeros((1, 1), F32), kept[0], kept[0] + kept[1]]
    kept_total = place[2] + kept[2]

    cut = one_if(count((CAP, ROWS), 1) == count((CAP, ROWS), 0) + BLOCK * kept_total)
    cut = cut.astype(BF16)
    loads[0].wait()
    pg[z] = dot(cut, gf[t, :ROWS, :]).astype(BF16)
    loads[1].wait()

    pl.semaphore_wait(barrier, 2 * NEAR + 1 + (NT - 1) + (NX - 1))

    def gather_z(buf, ss, rs, n):
        def msg(a, j, half=None):
            k = (a + j) % NZ
            sem = NZ if half == 1 else k
            ref = buf.at[zat(-a)]
            if half is not None:
                ref = ref.at[pl.ds(half * BLOCK, BLOCK)]
            return copy_to(ref, ref, ss.at[sem], rs.at[sem], dp=2 * zat(j) + c)

        def arrived(k, half=None):
            sem = NZ if half == 1 else k
            ref = buf.at[zat(-k)]
            if half is not None:
                ref = ref.at[pl.ds(half * BLOCK, BLOCK)]
            copy_to(ref, ref, ss.at[sem], rs.at[sem], dp=2 * zat(k) + c).wait_recv()

        def one():
            for j in (4, -4, 2, -2, 1, -1):
                go(msg(0, j))

        def two():
            arrived(4)
            go(msg(4, 4, 0))
            arrived(12)
            go(msg(-4, -4, 1))
            for j in (3, 2, 1, -1):
                go(msg(4, j))
                go(msg(-4, -j))

        def cross():
            return copy_to(give.at[n], got.at[n], sib_s.at[n], sib_r.at[n], dp=sibling)

        def pick(peer):
            acc = jnp.zeros((CAP, NARROW), BF16)
            for k in range(NZ):
                mark = one_if(peer == (c + 2 * k).astype(F32))
                acc = acc + buf[k] * jnp.broadcast_to(mark, (1, NARROW)).astype(BF16)
            return acc

        def three(other_peer):
            for k in (1, 15, 2, 14, 3, 13, 5, 11, 6, 10, 7, 9):
                arrived(k)
            arrived(8, 0)
            arrived(8, 1)
            give[n] = pick(other_peer)
            go(cross())

        def four(peer):
            acc = pick(peer)
            cross().wait_recv()
            return acc + got[n]

        return one, two, three, four

    zg = gather_z(pg, zg_s, zg_r, 0)
    za = gather_z(pa, za_s, za_r, 1)

    def ring_msg(step, way, buf, n, half):
        slot = yat(-way * (step - 1))
        ref = buf.at[slot, pl.ds(half * HALF, HALF)]
        sem = ((step - 1) * 2 + (way + 1) // 2) * 4 + n * 2 + half
        return copy_to(ref, ref, ring_s.at[sem], ring_r.at[sem], tensor=yat(way))

    def ring_sends(step):
        for half in range(2):
            for n, buf in enumerate((tf, gf)):
                for way in (1, -1):
                    if step < 4 or half == (1 - way) // 2:
                        go(ring_msg(step, way, buf, n, half))

    def ring_waits(step):
        for half in range(2):
            for n, buf in enumerate((tf, gf)):
                for way in (1, -1):
                    if step < 4 or half == (1 - way) // 2:
                        slot = yat(-way * step)
                        ref = buf.at[slot, pl.ds(half * HALF, HALF)]
                        sem = ((step - 1) * 2 + (way + 1) // 2) * 4 + n * 2 + half
                        copy_to(
                            ref, ref, ring_s.at[sem], ring_r.at[sem], tensor=yat(way)
                        ).wait_recv()
                        if step < 3 or (step == 3 and half == (1 - way) // 2):
                            go(ring_msg(step + 1, way, buf, n, half))

    zg[0]()
    ring_sends(1)
    ring_waits(1)
    zg[1]()
    ring_waits(2)
    ring_waits(3)
    zg[2](target_of(beside))

    gf[t, ROWS:, :] = zg[3](target_of(here))
    img_ref = gf.at[t, pl.ds(ROWS, CAP)]
    for k in (4, 3, 5, 2, 6, 1, 7):
        go(copy_to(img_ref, img_ref, img_s.at[k], img_r.at[k], tensor=yat(k)))
    ring_waits(4)

    loads[2].wait()
    loads[3].wait()
    tokens = jnp.concatenate([tf[n] for n in range(NT)], axis=1)
    for j in range(3):
        qkv[j] = dot(tokens, wi[j]).astype(BF16)

    lane = lax.broadcasted_iota(jnp.int32, (1, NARROW), 1)
    low = lane < BLOCK
    zero = jnp.zeros((), F32)

    def two_heads(x):
        x = x.astype(F32)
        return jnp.concatenate(
            [jnp.where(low, x, zero).astype(BF16), jnp.where(low, zero, x).astype(BF16)], axis=0
        )

    def one_head(x):
        return jnp.where(low, x[:CAP], x[CAP:])

    row = count((ROWS, 1), 0)
    column = jnp.full((ROWS, 1), -1.0, F32)
    for i in range(IMG):
        inside = one_if(row >= BLOCK * first[i]) * one_if(row < BLOCK * (first[i] + length[i]))
        shift = BLOCK * (stays[i] * place[i] + moved[i] * BLOCKS - first[i])
        column = column + inside * (row + shift + 1.0)
    move[...] = one_if(count((ROWS, EXTRA), 1) == column).astype(BF16)

    def image_of(position):
        marks = jnp.zeros(position.shape, F32)
        for edge in (first[1], first[2], total):
            marks = marks + one_if(position >= edge * BLOCK)
        return marks

    for i, start in enumerate(WINDOWS):
        place_in = count((2 * CAP, 1), 0)
        row_image = image_of(place_in - CAP * one_if(place_in >= CAP) + i * CAP)
        key_image = image_of(count((1, 2 * CAP), 1) + start)
        allowed = (row_image == key_image) & (row_image < IMG)
        query = two_heads(qkv[0, i * CAP : (i + 1) * CAP, :])
        scores = dot(query, qkv[1, start : start + 2 * CAP, :], 1, 1) * 0.125
        scores = jnp.where(allowed, scores, -1e30)
        peak = jnp.max(scores, axis=-1, keepdims=True)
        weights = jnp.where(allowed, jnp.exp(scores - peak), 0.0)
        totals = jnp.sum(weights, axis=-1, keepdims=True)
        totals = jnp.where(row_image < IMG, totals, 1.0)
        share = weights / totals
        shares[i] = share
        mixed = dot(share.astype(BF16), qkv[2, start : start + 2 * CAP, :])
        att[i * CAP : (i + 1) * CAP, :] = one_head(mixed).astype(BF16)

    attx[...] = dot(move[...], att[...], 0, 0).astype(BF16)
    pa[z] = attx[ROWS:, :]
    za[0]()

    for n in range(NT):
        tft[n] = tf[n].T
    cotangent = jnp.concatenate([gf[n, :ROWS, :] for n in range(NT)], axis=1)
    gax[:ROWS, :] = dot(cotangent, wo[...], 1, 1).astype(BF16)
    for n in range(NT):
        gowacc[n] = dot(attx[:ROWS, :], gf[n, :ROWS, :], 0, 0)

    for k in (1, 7, 2, 6, 3, 5, 4):
        ref = gf.at[yat(-k), pl.ds(ROWS, CAP)]
        copy_to(ref, ref, img_s.at[k], img_r.at[k], tensor=yat(k)).wait_recv()
    cotangent = jnp.concatenate([gf[n, ROWS:, :] for n in range(NT)], axis=1)
    gax[ROWS:, :] = dot(cotangent, wo[...], 1, 1).astype(BF16)
    ga[...] = dot(move[...], gax[...]).astype(BF16)

    gacc[...] = jnp.zeros(gacc.shape, F32)
    for i, start in enumerate(WINDOWS):
        window = slice(start, start + 2 * CAP)
        rows = slice(i * CAP, (i + 1) * CAP)
        share = shares[i]
        pull = two_heads(ga[rows, :])
        query = two_heads(qkv[0, rows, :])
        grad_share = dot(pull, qkv[2, window, :], 1, 1)
        inner = jnp.sum(share * grad_share, axis=-1, keepdims=True)
        grad_score = (0.125 * share * (grad_share - inner)).astype(BF16)
        gcat[rows, 0:NARROW] = one_head(dot(grad_score, qkv[1, window, :])).astype(BF16)
        gacc[0, window, :] += dot(grad_score, query, 0, 0)
        gacc[1, window, :] += dot(share.astype(BF16), pull, 0, 0)
    gcat[:, NARROW : 2 * NARROW] = gacc[0].astype(BF16)
    gcat[:, 2 * NARROW :] = gacc[1].astype(BF16)

    za[1]()

    mine = (3 - c, c)
    other = (2 + c, 1 - c)

    def core_msg(s):
        return copy_to(part.at[other[s]], crecv.at[s], core_s.at[s], core_r.at[s], dp=sibling)

    for n in range(NT):
        rows = slice(n * NARROW, (n + 1) * NARROW)
        part[2, rows, :] = dot(tft[n], gcat[:, 2 * NARROW :]).astype(BF16)
        part[3, rows, :] = (gowacc[n] + dot(attx[ROWS:, :], gf[n, ROWS:, :], 0, 0)).astype(BF16)
    go(core_msg(0))
    for n in range(NT):
        rows = slice(n * NARROW, (n + 1) * NARROW)
        grads = dot(tft[n], gcat[:, : 2 * NARROW])
        part[0, rows, :] = grads[:, :NARROW].astype(BF16)
        part[1, rows, :] = grads[:, NARROW:].astype(BF16)
    go(core_msg(1))

    def reduce_y(buf, land, which):
        def plan(kind, way):
            w = (1 - way) // 2
            half = pl.ds(w * HALF, HALF)
            if kind == 0:
                return buf.at[yat(3 * way)], land.at[w], w, way
            if kind == 1:
                return buf.at[yat(4 * way), half], land.at[2, half], 2 + w, 2 * way
            if kind == 2:
                return buf.at[yat(way)], land.at[3 + w], 4 + w, way
            return buf.at[yat(2 * way)], land.at[5 + w], 6 + w, 2 * way

        def msg(kind, way):
            src, dst, sem, hop = plan(kind, way)
            sem = which * 8 + sem
            return copy_to(src, dst, rs_s.at[sem], rs_r.at[sem], tensor=yat(hop))

        def begin():
            for kind in (1, 0, 2):
                for way in (1, -1):
                    go(msg(kind, way))

        def middle():
            for way in (1, -1):
                w = (1 - way) // 2
                msg(0, way).wait_recv()
                msg(1, way).wait_recv()
                for half in range(2):
                    rows = slice(half * HALF, (half + 1) * HALF)
                    acc = buf[yat(2 * way), rows, :].astype(F32) + land[w, rows, :].astype(F32)
                    if half == w:
                        acc = acc + land[2, rows, :].astype(F32)
                    buf[yat(2 * way), rows, :] = acc.astype(BF16)
                go(msg(3, way))

        def last(out):
            acc = buf[t].astype(F32)
            for kind in (2, 3):
                for way in (1, -1):
                    msg(kind, way).wait_recv()
                    acc = acc + land[2 * kind - 1 + (1 - way) // 2].astype(F32)
            out[...] = acc.astype(BF16)

        return begin, middle, last

    back = reduce_y(pback, rback, 0)
    outs = reduce_y(pout, rout, 1)

    def core_sum(s):
        core_msg(s).wait_recv()
        csum[s] = (part[mine[s]].astype(F32) + crecv[s].astype(F32)).astype(BF16)

    def xr_msg(s, k):
        peer = xat(k)
        return copy_to(
            csum.at[s, pl.ds(pl.multiple_of(peer * 256, 256), 256)],
            xrecv.at[s, k - 1],
            xr_s.at[s, k],
            xr_r.at[s, k],
            outer=peer,
        )

    def x_send(s):
        for k in (2, 1, 3):
            go(xr_msg(s, k))

    def x_sum(s):
        for k in (1, 3, 2):
            xr_msg(s, k).wait_recv()
        acc = csum[s, pl.ds(pl.multiple_of(o * 256, 256), 256), :].astype(F32)
        for k in range(3):
            acc = acc + xrecv[s, k].astype(F32)
        tsum[s] = acc.astype(BF16)

    def far_first(m):
        half = lax.div(m + 1, 2)
        return 8 + half * (1 - 2 * lax.rem(m, 2))

    def zr_msg(s, k):
        peer = lax.rem(z + k, NZ)
        return copy_to(
            tsum.at[s, pl.ds(pl.multiple_of(peer * 16, 16), 16)],
            zrecv.at[s, k],
            zr_s.at[s, k],
            zr_r.at[s, k],
            dp=2 * peer + c,
        )

    def z_rows(place_z):
        return pl.ds(pl.multiple_of(o * 256 + place_z * 16, 16), 16)

    def zb_msg(s, k):
        peer = lax.rem(z + k, NZ)
        ref = full.at[mine[s], z_rows(z)]
        return copy_to(ref, ref, zb_s.at[s, k], zb_r.at[s, k], dp=2 * peer + c)

    def each_z(fn):
        def body(m, carry):
            fn(far_first(m))
            return carry

        lax.fori_loop(0, NZ - 1, body, 0)

    def z_send(s):
        each_z(lambda k: zr_msg(s, k).start())

    def z_sum(s):
        each_z(lambda k: zr_msg(s, k).wait_recv())
        acc = tsum[s, pl.ds(pl.multiple_of(z * 16, 16), 16), :].astype(F32)
        for k in range(1, NZ):
            acc = acc + zrecv[s, k].astype(F32)
        full[mine[s], z_rows(z), :] = acc.astype(BF16)
        each_z(lambda k: zb_msg(s, k).start())

    def xb_msg(s, k):
        ref = full.at[mine[s], pl.ds(pl.multiple_of(o * 256, 256), 256)]
        return copy_to(ref, ref, xb_s.at[s, k], xb_r.at[s, k], outer=xat(k))

    def xb_wait(s, k):
        ref = full.at[mine[s], pl.ds(pl.multiple_of(xat(NX - k) * 256, 256), 256)]
        copy_to(ref, ref, xb_s.at[s, k], xb_r.at[s, k], outer=xat(k)).wait_recv()

    def cb_msg(s, k):
        ref = full.at[mine[s], pl.ds(pl.multiple_of(xat(NX - k) * 256, 256), 256)]
        return copy_to(ref, ref, cb_s.at[s, k], cb_r.at[s, k], dp=sibling)

    def cb_wait(s, k):
        ref = full.at[other[s], pl.ds(pl.multiple_of(xat(NX - k) * 256, 256), 256)]
        copy_to(ref, ref, cb_s.at[s, k], cb_r.at[s, k], dp=sibling).wait_recv()

    def z_got(s, k):
        ref = full.at[mine[s], z_rows(lax.rem(z + (NZ - k), NZ))]
        peer = lax.rem(z + k, NZ)
        copy_to(ref, ref, zb_s.at[s, k], zb_r.at[s, k], dp=2 * peer + c).wait_recv()

    def spread_x(s):
        each_z(lambda k: z_got(s, k))
        for k in (2, 1, 3):
            go(xb_msg(s, k))
        go(cb_msg(s, 0))

    def spread_core(s):
        for k in (1, 3, 2):
            xb_wait(s, k)
            go(cb_msg(s, k))

    core_sum(0)
    x_send(0)
    core_sum(1)
    x_send(1)

    for n in range(NT):
        weight = jnp.concatenate([wi[j, n * NARROW : (n + 1) * NARROW, :] for j in range(3)], axis=1)
        pback[n] = dot(gcat[...], weight, 1, 1).astype(BF16)
    back[0]()
    x_sum(0)
    z_send(0)
    x_sum(1)
    z_send(1)
    za[2](source_of(beside))
    back[1]()

    in_len = jnp.sum(
        jnp.sum(coming_to(here) * blocks_all, axis=1, keepdims=True), axis=0, keepdims=True
    )
    put_row, put_col = count((ROWS, CAP), 0), count((ROWS, CAP), 1)
    put = one_if(put_row == put_col + BLOCK * kept_total) * one_if(put_col < BLOCK * in_len)
    incoming = dot(put.astype(BF16), za[3](source_of(here)))
    att[...] = (attx[:ROWS, :].astype(F32) + incoming).astype(BF16)
    for n in range(NT):
        pout[n] = dot(att[...], wo[:, n * NARROW : (n + 1) * NARROW]).astype(BF16)
    outs[0]()
    z_sum(0)
    z_sum(1)
    outs[1]()
    stores = []

    def keep(src, dst):
        cp = pltpu.make_async_copy(src, dst, store.at[len(stores)])
        cp.start()
        stores.append(cp)

    def keep_piece(chunk, k):
        rows = pl.ds(pl.multiple_of(xat(NX - k) * 256, 256), 256)
        keep(full.at[chunk, rows], sum_o.at[chunk, rows])

    back[2](gtok)
    keep(gtok, gtok_o)
    spread_x(0)
    spread_x(1)
    outs[2](lay)
    keep(lay, lay_o)
    for s in range(2):
        spread_core(s)
        for k in range(NX):
            keep_piece(mine[s], k)
    for s in range(2):
        for k in (0, 1, 3, 2):
            cb_wait(s, k)
            keep_piece(other[s], k)

    for cp in pending:
        cp.wait_send()
    for s in range(2):
        each_z(lambda k: zr_msg(s, k).wait_send())
        each_z(lambda k: zb_msg(s, k).wait_send())
    for cp in stores:
        cp.wait()


def finish(
    lay_i, gtok_i, sum_i, lay_o, gtok_o, giw_o, gow_o, low, wide, flat, lay, gtok, sem_i, sem_o
):
    reads = [pltpu.make_async_copy(sum_i.at[j], low.at[j], sem_i.at[j]) for j in range(4)]
    reads.append(pltpu.make_async_copy(lay_i, lay, sem_i.at[4]))
    reads.append(pltpu.make_async_copy(gtok_i, gtok, sem_i.at[5]))
    copies = []
    for cp in reads:
        cp.start()
    for j in range(3):
        reads[j].wait()
        wide[j] = low[j].astype(F32)
        copies.append(pltpu.make_async_copy(wide.at[j], giw_o.at[j], sem_o.at[j]))
        copies[-1].start()
    reads[3].wait()
    for n in range(NT):
        columns = slice(n * NARROW, (n + 1) * NARROW)
        flat[:, columns] = low[3, columns, :].astype(F32)
    copies.append(pltpu.make_async_copy(flat, gow_o, sem_o.at[3]))
    copies[-1].start()
    for j, src, dst in ((4, lay, lay_o), (5, gtok, gtok_o)):
        reads[j].wait()
        copies.append(pltpu.make_async_copy(src, dst, sem_o.at[j]))
        copies[-1].start()
    for cp in copies:
        cp.wait()


def on_device(tokens, input_weight, output_weight, grad_layer, patch_blocks, target_group):
    vmem = pl.BlockSpec(memory_space=pltpu.VMEM)
    hbm = pl.BlockSpec(memory_space=pl.ANY)
    dma = pltpu.SemaphoreType.DMA

    def buf(*shape, dtype=BF16):
        return pltpu.VMEM(shape, dtype)

    rows_bf16 = jax.ShapeDtypeStruct((ROWS, NARROW), BF16)
    layer_out, grad_tokens, sums = pl.pallas_call(
        kernel,
        out_shape=(rows_bf16, rows_bf16, jax.ShapeDtypeStruct((4, NT * NARROW, NARROW), BF16)),
        in_specs=[hbm] * 4 + [vmem] * 2,
        out_specs=(hbm,) * 3,
        scratch_shapes=[
            buf(3, 1024, NARROW),
            buf(NARROW, 1024),
            buf(NT, ROWS, NARROW),
            buf(NT, NARROW, ROWS),
            buf(NT, EXTRA, NARROW),
            buf(NZ, CAP, NARROW),
            buf(NZ, CAP, NARROW),
            buf(2, CAP, NARROW),
            buf(2, CAP, NARROW),
            buf(ROWS, EXTRA),
            buf(3, ROWS, NARROW),
            buf(ROWS, NARROW),
            buf(EXTRA, NARROW),
            buf(3, 2 * CAP, 2 * CAP, dtype=F32),
            buf(ROWS, NARROW),
            buf(EXTRA, NARROW),
            buf(ROWS, 3 * NARROW),
            buf(2, ROWS, NARROW, dtype=F32),
            buf(NT, NARROW, NARROW, dtype=F32),
            buf(ROWS, NARROW),
            buf(ROWS, NARROW),
            buf(4, 1024, NARROW),
            buf(2, 1024, NARROW),
            buf(2, 1024, NARROW),
            buf(2, 3, 256, NARROW),
            buf(2, 256, NARROW),
            buf(2, NZ, 16, NARROW),
            buf(4, 1024, NARROW),
            buf(NT, ROWS, NARROW),
            buf(NT, ROWS, NARROW),
            buf(7, ROWS, NARROW),
            buf(7, ROWS, NARROW),
            dma((32,)), dma((32,)),
            dma((NT,)), dma((NT,)),
            dma((NZ + 1,)), dma((NZ + 1,)),
            dma((NZ + 1,)), dma((NZ + 1,)),
            dma((2,)), dma((2,)),
            dma((4,)), dma((18,)),
            dma((2,)), dma((2,)),
            dma((2, NX)), dma((2, NX)),
            dma((2, NZ)), dma((2, NZ)),
            dma((2, NZ)), dma((2, NZ)),
            dma((2, NX)), dma((2, NX)),
            dma((2, NX)), dma((2, NX)),
            dma((16,)), dma((16,)),
        ],
        compiler_params=pltpu.CompilerParams(
            collective_id=0, has_side_effects=True, vmem_limit_bytes=56 * 2**20
        ),
    )(
        tokens,
        jnp.transpose(input_weight, (1, 0, 2)),
        output_weight,
        grad_layer,
        patch_blocks.T,
        target_group.T,
    )
    layer_out, grad_tokens, input_sum, output_sum = pl.pallas_call(
        finish,
        out_shape=(
            rows_bf16,
            rows_bf16,
            jax.ShapeDtypeStruct((3, NT * NARROW, NARROW), F32),
            jax.ShapeDtypeStruct((NARROW, NT * NARROW), F32),
        ),
        in_specs=[hbm] * 3,
        out_specs=(hbm,) * 4,
        scratch_shapes=[
            buf(4, NT * NARROW, NARROW),
            buf(3, NT * NARROW, NARROW, dtype=F32),
            buf(NARROW, NT * NARROW, dtype=F32),
            buf(ROWS, NARROW),
            buf(ROWS, NARROW),
            dma((6,)),
            dma((6,)),
        ],
        compiler_params=pltpu.CompilerParams(vmem_limit_bytes=56 * 2**20),
    )(layer_out, grad_tokens, sums)
    return layer_out, grad_tokens, jnp.transpose(input_sum, (1, 0, 2)), output_sum


def solution(mesh):
    return jax.shard_map(
        on_device,
        mesh=mesh,
        in_specs=(
            P(("outer", "dp"), "tensor"),
            P(None, None, "tensor"),
            P("tensor", None),
            P(("outer", "dp"), "tensor"),
            P(),
            P(),
        ),
        out_specs=(
            P(("outer", "dp"), "tensor"),
            P(("outer", "dp"), "tensor"),
            P(None, None, "tensor"),
            P("tensor", None),
        ),
        check_vma=False,
    )
```

```python
import jax
import jax.numpy as jnp
from jax import lax
from jax.experimental import pallas as pl
from jax.experimental.pallas import tpu as pltpu
from jax.sharding import PartitionSpec as P

MESH = pl.DeviceIdType.MESH
BF16 = jnp.bfloat16
F32 = jnp.float32

ROWS = 384
NARROW = 128
BLOCK = 64
BLOCKS = 6
IMG = 3
CAP = 128
NT = 8
NZ = 16
NX = 4
NDP = 32
NEAR = 4
HALF = ROWS // 2
EXTRA = ROWS + CAP
WINDOWS = (0, 64, 128)


def dot(a, b, ca=1, cb=0):
    return lax.dot_general(a, b, (((ca,), (cb,)), ((), ())), preferred_element_type=F32)


def one_if(condition):
    return jnp.where(condition, 1.0, 0.0)


def count(shape, axis):
    return lax.broadcasted_iota(jnp.int32, shape, axis).astype(F32)


def copy_to(src, dst, send, recv, **device):
    return pltpu.make_async_remote_copy(
        src_ref=src,
        dst_ref=dst,
        send_sem=send,
        recv_sem=recv,
        device_id=device,
        device_id_type=MESH,
    )


def kernel(
    tok, wi_hbm, wo_hbm, gl, pb, tg,
    lay_o, gtok_o, sum_o,
    wi, wo, tf, tft, gf, pg, pa, give, got, move, qkv, ga, gax, shares, att, attx, gcat, gacc, qacc, gaacc, gowacc, wacc, hand, thand, hshare, ghand,
    lay, gtok, part, csum, crecv, xrecv, tsum, zrecv, full,
    pback, pout, rback, rout,
    ring_s, ring_r, img_s, img_r, zg_s, zg_r, za_s, za_r, sib_s, sib_r,
    load, store, core_s, core_r, xr_s, xr_r, zr_s, zr_r, zb_s, zb_r, xb_s, xb_r, cb_s, cb_r,
    rs_s, rs_r,
):
    o = lax.axis_index("outer")
    d = lax.axis_index("dp")
    t = lax.axis_index("tensor")
    z = lax.div(d, 2)
    c = lax.rem(d, 2)
    sibling = d + 1 - 2 * c

    def yat(k):
        return lax.rem(t + (k + NT), NT)

    def zat(k):
        return lax.rem(z + (k + NZ), NZ)

    def xat(k):
        return lax.rem(o + k, NX)

    pending = []

    def go(cp):
        cp.start()
        pending.append(cp)

    loads = [
        pltpu.make_async_copy(gl, gf.at[t, pl.ds(0, ROWS)], load.at[0]),
        pltpu.make_async_copy(tok, tf.at[t], load.at[1]),
        pltpu.make_async_copy(wi_hbm, wi, load.at[2]),
        pltpu.make_async_copy(wo_hbm, wo, load.at[3]),
    ]
    for cp in loads:
        cp.start()

    barrier = pltpu.get_barrier_semaphore()

    def greet(**device):
        pl.semaphore_signal(barrier, inc=1, device_id=device, device_id_type=MESH)

    for k in range(1, NEAR + 1):
        greet(dp=2 * zat(k) + c)
        greet(dp=2 * zat(-k) + c)
    greet(dp=sibling)
    for k in range(1, NT):
        greet(tensor=yat(k))
    for k in range(1, NX):
        greet(outer=xat(k))

    here = d.astype(F32)
    beside = sibling.astype(F32)
    lane3 = count((IMG, NARROW), 1)
    blocks_all = pb[...].astype(F32)
    dest_all = tg[...].astype(F32)

    def own_of(table, owner):
        mark = one_if(lane3 == (o * NDP).astype(F32) + owner)
        return jnp.sum(table * mark, axis=1, keepdims=True)

    def target_of(owner):
        takers = own_of(dest_all, owner)
        return jnp.sum(takers * one_if(takers != owner), axis=0, keepdims=True)

    def coming_to(owner):
        base = (o * NDP).astype(F32)
        mark = one_if(dest_all == owner) * one_if(lane3 != base + owner)
        return mark * one_if(lane3 >= base) * one_if(lane3 < base + NDP)

    def source_of(owner):
        marks = coming_to(owner) * (lane3 - (o * NDP).astype(F32))
        return jnp.sum(jnp.sum(marks, axis=1, keepdims=True), axis=0, keepdims=True)

    length3 = own_of(blocks_all, here)
    dest3 = own_of(dest_all, here)
    length = [length3[i : i + 1] for i in range(IMG)]
    dest = [dest3[i : i + 1] for i in range(IMG)]
    first = [jnp.zeros((1, 1), F32), length[0], length[0] + length[1]]
    total = first[2] + length[2]
    stays = [one_if(dest[i] == here) for i in range(IMG)]
    moved = [1.0 - stays[i] for i in range(IMG)]
    kept = [stays[i] * length[i] for i in range(IMG)]
    place = [jnp.zeros((1, 1), F32), kept[0], kept[0] + kept[1]]
    kept_total = place[2] + kept[2]

    cut = one_if(count((CAP, ROWS), 1) == count((CAP, ROWS), 0) + BLOCK * kept_total)
    cut = cut.astype(BF16)
    loads[0].wait()
    pg[z] = dot(cut, gf[t, :ROWS, :]).astype(BF16)
    loads[1].wait()

    pl.semaphore_wait(barrier, 2 * NEAR + 1 + (NT - 1) + (NX - 1))

    def gather_z(buf, ss, rs, n):
        def msg(a, j, half=None):
            k = (a + j) % NZ
            sem = NZ if half == 1 else k
            ref = buf.at[zat(-a)]
            if half is not None:
                ref = ref.at[pl.ds(half * BLOCK, BLOCK)]
            return copy_to(ref, ref, ss.at[sem], rs.at[sem], dp=2 * zat(j) + c)

        def arrived(k, half=None):
            sem = NZ if half == 1 else k
            ref = buf.at[zat(-k)]
            if half is not None:
                ref = ref.at[pl.ds(half * BLOCK, BLOCK)]
            copy_to(ref, ref, ss.at[sem], rs.at[sem], dp=2 * zat(k) + c).wait_recv()

        def one():
            for j in (4, -4, 2, -2, 1, -1):
                go(msg(0, j))

        def two():
            arrived(4)
            go(msg(4, 4, 0))
            arrived(12)
            go(msg(-4, -4, 1))
            for j in (3, 2, 1, -1):
                go(msg(4, j))
                go(msg(-4, -j))

        def cross():
            return copy_to(give.at[n], got.at[n], sib_s.at[n], sib_r.at[n], dp=sibling)

        def pick(peer):
            acc = jnp.zeros((CAP, NARROW), BF16)
            for k in range(NZ):
                mark = one_if(peer == (c + 2 * k).astype(F32))
                acc = acc + buf[k] * jnp.broadcast_to(mark, (1, NARROW)).astype(BF16)
            return acc

        def three(other_peer):
            for k in (1, 15, 2, 14, 3, 13, 5, 11, 6, 10, 7, 9):
                arrived(k)
            arrived(8, 0)
            arrived(8, 1)
            give[n] = pick(other_peer)
            go(cross())

        def four(peer):
            acc = pick(peer)
            cross().wait_recv()
            return acc + got[n]

        return one, two, three, four

    zg = gather_z(pg, zg_s, zg_r, 0)
    za = gather_z(pa, za_s, za_r, 1)

    def ring_msg(step, way, buf, n, half):
        slot = yat(-way * (step - 1))
        ref = buf.at[slot, pl.ds(half * HALF, HALF)]
        sem = ((step - 1) * 2 + (way + 1) // 2) * 4 + n * 2 + half
        return copy_to(ref, ref, ring_s.at[sem], ring_r.at[sem], tensor=yat(way))

    def ring_sends(step):
        for half in range(2):
            for n, buf in enumerate((tf, gf)):
                for way in (1, -1):
                    if step < 4 or half == (1 - way) // 2:
                        go(ring_msg(step, way, buf, n, half))

    def ring_waits(step):
        for half in range(2):
            for n, buf in enumerate((tf, gf)):
                for way in (1, -1):
                    if step < 4 or half == (1 - way) // 2:
                        slot = yat(-way * step)
                        ref = buf.at[slot, pl.ds(half * HALF, HALF)]
                        sem = ((step - 1) * 2 + (way + 1) // 2) * 4 + n * 2 + half
                        copy_to(
                            ref, ref, ring_s.at[sem], ring_r.at[sem], tensor=yat(way)
                        ).wait_recv()
                        if step < 3 or (step == 3 and half == (1 - way) // 2):
                            go(ring_msg(step + 1, way, buf, n, half))

    zg[0]()
    ring_sends(1)
    ring_waits(1)
    zg[1]()
    ring_waits(2)

    row = count((ROWS, 1), 0)
    column = jnp.full((ROWS, 1), -1.0, F32)
    for i in range(IMG):
        inside = one_if(row >= BLOCK * first[i]) * one_if(row < BLOCK * (first[i] + length[i]))
        shift = BLOCK * (stays[i] * place[i] + moved[i] * BLOCKS - first[i])
        column = column + inside * (row + shift + 1.0)
    move[...] = one_if(count((ROWS, EXTRA), 1) == column).astype(BF16)

    def columns_of(slot):
        return pl.ds(pl.multiple_of(slot * NARROW, NARROW), NARROW)

    def project(offsets, begin):
        slots = [yat(k) for k in offsets]
        shard = jnp.concatenate([tf[slot] for slot in slots], axis=1)
        weight = jnp.concatenate(
            [
                jnp.concatenate([wi[j, columns_of(slot), :] for j in range(3)], axis=1)
                for slot in slots
            ],
            axis=0,
        )
        term = dot(shard, weight)
        qacc[...] = term if begin else qacc[...] + term
        shard = jnp.concatenate([gf[slot, :ROWS, :] for slot in slots], axis=1)
        weight = jnp.concatenate([wo[:, columns_of(slot)] for slot in slots], axis=1)
        term = dot(shard, weight, 1, 1)
        gaacc[...] = term if begin else gaacc[...] + term
        for slot in slots:
            tft[slot] = tf[slot].T

    loads[2].wait()
    loads[3].wait()
    project((0, 1, -1, 2, -2), True)
    ring_waits(3)
    project((3, -3), False)
    zg[2](target_of(beside))

    gf[t, ROWS:, :] = zg[3](target_of(here))
    img_ref = gf.at[t, pl.ds(ROWS, CAP)]
    for k in (4, 3, 5, 2, 6, 1, 7):
        go(copy_to(img_ref, img_ref, img_s.at[k], img_r.at[k], tensor=yat(k)))
    ring_waits(4)

    project((4,), False)
    for j in range(3):
        qkv[j] = qacc[:, j * NARROW : (j + 1) * NARROW].astype(BF16)

    lane = lax.broadcasted_iota(jnp.int32, (1, NARROW), 1)
    low = lane < BLOCK
    zero = jnp.zeros((), F32)

    def two_heads(x):
        x = x.astype(F32)
        return jnp.concatenate(
            [jnp.where(low, x, zero).astype(BF16), jnp.where(low, zero, x).astype(BF16)], axis=0
        )

    def one_head(x):
        return jnp.where(low, x[:CAP], x[CAP:])

    def image_of(position):
        marks = jnp.zeros(position.shape, F32)
        for edge in (first[1], first[2], total):
            marks = marks + one_if(position >= edge * BLOCK)
        return marks

    for i, start in enumerate(WINDOWS):
        place_in = count((2 * CAP, 1), 0)
        row_image = image_of(place_in - CAP * one_if(place_in >= CAP) + i * CAP)
        key_image = image_of(count((1, 2 * CAP), 1) + start)
        allowed = (row_image == key_image) & (row_image < IMG)
        query = two_heads(qkv[0, i * CAP : (i + 1) * CAP, :])
        scores = dot(query, qkv[1, start : start + 2 * CAP, :], 1, 1) * 0.125
        scores = jnp.where(allowed, scores, -1e30)
        peak = jnp.max(scores, axis=-1, keepdims=True)
        weights = jnp.where(allowed, jnp.exp(scores - peak), 0.0)
        totals = jnp.sum(weights, axis=-1, keepdims=True)
        totals = jnp.where(row_image < IMG, totals, 1.0)
        share = weights / totals
        shares[i] = share
        mixed = dot(share.astype(BF16), qkv[2, start : start + 2 * CAP, :])
        att[i * CAP : (i + 1) * CAP, :] = one_head(mixed).astype(BF16)

    attx[...] = dot(move[...], att[...], 0, 0).astype(BF16)
    pa[z] = attx[ROWS:, :]
    za[0]()

    gax[...] = gaacc[...].astype(BF16)
    for n in range(NT):
        gowacc[n] = dot(attx[:ROWS, :], gf[n, :ROWS, :], 0, 0)
    ga[...] = dot(move[:, :ROWS], gax[...]).astype(BF16)

    gacc[...] = jnp.zeros(gacc.shape, F32)
    for i, start in enumerate(WINDOWS):
        window = slice(start, start + 2 * CAP)
        rows = slice(i * CAP, (i + 1) * CAP)
        share = shares[i]
        pull = two_heads(ga[rows, :])
        query = two_heads(qkv[0, rows, :])
        grad_share = dot(pull, qkv[2, window, :], 1, 1)
        inner = jnp.sum(share * grad_share, axis=-1, keepdims=True)
        grad_score = (0.125 * share * (grad_share - inner)).astype(BF16)
        gcat[rows, 0:NARROW] = one_head(dot(grad_score, qkv[1, window, :])).astype(BF16)
        gacc[0, window, :] += dot(grad_score, query, 0, 0)
        gacc[1, window, :] += dot(share.astype(BF16), pull, 0, 0)
    gcat[:, NARROW : 2 * NARROW] = gacc[0].astype(BF16)
    gcat[:, 2 * NARROW :] = gacc[1].astype(BF16)

    for n in range(NT):
        grads = dot(tft[n], gcat[...])
        for j in range(3):
            wacc[j, n * NARROW : (n + 1) * NARROW, :] = grads[:, j * NARROW : (j + 1) * NARROW]

    lift = move[:, ROWS:]
    for j in range(3):
        hand[j] = dot(lift, qkv[j], 0, 0).astype(BF16)
    for n in range(NT):
        thand[n] = dot(tft[n], lift).astype(BF16)
    rows_handed = BLOCK * (moved[0] * length[0] + moved[1] * length[1] + moved[2] * length[2])
    place_in = count((2 * CAP, 1), 0)
    row_ok = place_in - CAP * one_if(place_in >= CAP) < rows_handed
    allowed = row_ok & (count((1, CAP), 1) < rows_handed)
    scores = dot(two_heads(hand[0]), hand[1], 1, 1) * 0.125
    scores = jnp.where(allowed, scores, -1e30)
    weights = jnp.where(allowed, jnp.exp(scores - jnp.max(scores, axis=-1, keepdims=True)), 0.0)
    totals = jnp.sum(weights, axis=-1, keepdims=True)
    hshare[...] = weights / jnp.where(row_ok, totals, 1.0)


    for k in (1, 7, 2, 6, 3, 5, 4):
        ref = gf.at[yat(-k), pl.ds(ROWS, CAP)]
        copy_to(ref, ref, img_s.at[k], img_r.at[k], tensor=yat(k)).wait_recv()
    cotangent = jnp.concatenate([gf[n, ROWS:, :] for n in range(NT)], axis=1)
    share = hshare[...]
    pull = two_heads(dot(cotangent, wo[...], 1, 1).astype(BF16))
    grad_share = dot(pull, hand[2], 1, 1)
    inner = jnp.sum(share * grad_share, axis=-1, keepdims=True)
    grad_score = (0.125 * share * (grad_share - inner)).astype(BF16)
    ghand[:, :NARROW] = one_head(dot(grad_score, hand[1])).astype(BF16)
    ghand[:, NARROW : 2 * NARROW] = dot(grad_score, two_heads(hand[0]), 0, 0).astype(BF16)
    ghand[:, 2 * NARROW :] = dot(share.astype(BF16), pull, 0, 0).astype(BF16)

    mine = (3 - c, c)
    other = (2 + c, 1 - c)

    def core_msg(s):
        return copy_to(part.at[other[s]], crecv.at[s], core_s.at[s], core_r.at[s], dp=sibling)

    for n in range(NT):
        rows = slice(n * NARROW, (n + 1) * NARROW)
        part[2, rows, :] = (wacc[2, rows, :] + dot(thand[n], ghand[:, 2 * NARROW :])).astype(BF16)
        part[3, rows, :] = (gowacc[n] + dot(attx[ROWS:, :], gf[n, ROWS:, :], 0, 0)).astype(BF16)
    go(core_msg(0))
    for n in range(NT):
        rows = slice(n * NARROW, (n + 1) * NARROW)
        grads = dot(thand[n], ghand[:, : 2 * NARROW])
        part[0, rows, :] = (wacc[0, rows, :] + grads[:, :NARROW]).astype(BF16)
        part[1, rows, :] = (wacc[1, rows, :] + grads[:, NARROW:]).astype(BF16)
    go(core_msg(1))
    za[1]()

    def reduce_y(buf, land, which):
        def plan(kind, way):
            w = (1 - way) // 2
            half = pl.ds(w * HALF, HALF)
            if kind == 0:
                return buf.at[yat(3 * way)], land.at[w], w, way
            if kind == 1:
                return buf.at[yat(4 * way), half], land.at[2, half], 2 + w, 2 * way
            if kind == 2:
                return buf.at[yat(way)], land.at[3 + w], 4 + w, way
            return buf.at[yat(2 * way)], land.at[5 + w], 6 + w, 2 * way

        def msg(kind, way):
            src, dst, sem, hop = plan(kind, way)
            sem = which * 8 + sem
            return copy_to(src, dst, rs_s.at[sem], rs_r.at[sem], tensor=yat(hop))

        def begin():
            for kind in (1, 0, 2):
                for way in (1, -1):
                    go(msg(kind, way))

        def middle():
            for way in (1, -1):
                w = (1 - way) // 2
                msg(0, way).wait_recv()
                msg(1, way).wait_recv()
                for half in range(2):
                    rows = slice(half * HALF, (half + 1) * HALF)
                    acc = buf[yat(2 * way), rows, :].astype(F32) + land[w, rows, :].astype(F32)
                    if half == w:
                        acc = acc + land[2, rows, :].astype(F32)
                    buf[yat(2 * way), rows, :] = acc.astype(BF16)
                go(msg(3, way))

        def last(out):
            acc = buf[t].astype(F32)
            for kind in (2, 3):
                for way in (1, -1):
                    msg(kind, way).wait_recv()
                    acc = acc + land[2 * kind - 1 + (1 - way) // 2].astype(F32)
            out[...] = acc.astype(BF16)

        return begin, middle, last

    back = reduce_y(pback, rback, 0)
    outs = reduce_y(pout, rout, 1)

    def core_sum(s):
        core_msg(s).wait_recv()
        csum[s] = (part[mine[s]].astype(F32) + crecv[s].astype(F32)).astype(BF16)

    def xr_msg(s, k):
        peer = xat(k)
        return copy_to(
            csum.at[s, pl.ds(pl.multiple_of(peer * 256, 256), 256)],
            xrecv.at[s, k - 1],
            xr_s.at[s, k],
            xr_r.at[s, k],
            outer=peer,
        )

    def x_send(s):
        for k in (2, 1, 3):
            go(xr_msg(s, k))

    def x_sum(s):
        for k in (1, 3, 2):
            xr_msg(s, k).wait_recv()
        acc = csum[s, pl.ds(pl.multiple_of(o * 256, 256), 256), :].astype(F32)
        for k in range(3):
            acc = acc + xrecv[s, k].astype(F32)
        tsum[s] = acc.astype(BF16)

    def far_first(m):
        half = lax.div(m + 1, 2)
        return 8 + half * (1 - 2 * lax.rem(m, 2))

    def zr_msg(s, k):
        peer = lax.rem(z + k, NZ)
        return copy_to(
            tsum.at[s, pl.ds(pl.multiple_of(peer * 16, 16), 16)],
            zrecv.at[s, k],
            zr_s.at[s, k],
            zr_r.at[s, k],
            dp=2 * peer + c,
        )

    def z_rows(place_z):
        return pl.ds(pl.multiple_of(o * 256 + place_z * 16, 16), 16)

    def zb_msg(s, k):
        peer = lax.rem(z + k, NZ)
        ref = full.at[mine[s], z_rows(z)]
        return copy_to(ref, ref, zb_s.at[s, k], zb_r.at[s, k], dp=2 * peer + c)

    def each_z(fn):
        def body(m, carry):
            fn(far_first(m))
            return carry

        lax.fori_loop(0, NZ - 1, body, 0)

    def z_send(s):
        each_z(lambda k: zr_msg(s, k).start())

    def z_sum(s):
        each_z(lambda k: zr_msg(s, k).wait_recv())
        acc = tsum[s, pl.ds(pl.multiple_of(z * 16, 16), 16), :].astype(F32)
        for k in range(1, NZ):
            acc = acc + zrecv[s, k].astype(F32)
        full[mine[s], z_rows(z), :] = acc.astype(BF16)
        each_z(lambda k: zb_msg(s, k).start())

    def xb_msg(s, k):
        ref = full.at[mine[s], pl.ds(pl.multiple_of(o * 256, 256), 256)]
        return copy_to(ref, ref, xb_s.at[s, k], xb_r.at[s, k], outer=xat(k))

    def xb_wait(s, k):
        ref = full.at[mine[s], pl.ds(pl.multiple_of(xat(NX - k) * 256, 256), 256)]
        copy_to(ref, ref, xb_s.at[s, k], xb_r.at[s, k], outer=xat(k)).wait_recv()

    def cb_msg(s, k):
        ref = full.at[mine[s], pl.ds(pl.multiple_of(xat(NX - k) * 256, 256), 256)]
        return copy_to(ref, ref, cb_s.at[s, k], cb_r.at[s, k], dp=sibling)

    def cb_wait(s, k):
        ref = full.at[other[s], pl.ds(pl.multiple_of(xat(NX - k) * 256, 256), 256)]
        copy_to(ref, ref, cb_s.at[s, k], cb_r.at[s, k], dp=sibling).wait_recv()

    def z_got(s, k):
        ref = full.at[mine[s], z_rows(lax.rem(z + (NZ - k), NZ))]
        peer = lax.rem(z + k, NZ)
        copy_to(ref, ref, zb_s.at[s, k], zb_r.at[s, k], dp=2 * peer + c).wait_recv()

    def spread_x(s):
        each_z(lambda k: z_got(s, k))
        for k in (2, 1, 3):
            go(xb_msg(s, k))
        go(cb_msg(s, 0))

    def spread_core(s):
        for k in (1, 3, 2):
            xb_wait(s, k)
            go(cb_msg(s, k))

    core_sum(0)
    x_send(0)
    core_sum(1)
    x_send(1)

    gcat[...] = (gcat[...].astype(F32) + dot(move[:, ROWS:], ghand[...])).astype(BF16)
    for n in range(NT):
        weight = jnp.concatenate([wi[j, n * NARROW : (n + 1) * NARROW, :] for j in range(3)], axis=1)
        pback[n] = dot(gcat[...], weight, 1, 1).astype(BF16)
    back[0]()
    x_sum(0)
    z_send(0)
    x_sum(1)
    z_send(1)
    za[2](source_of(beside))
    back[1]()

    in_len = jnp.sum(
        jnp.sum(coming_to(here) * blocks_all, axis=1, keepdims=True), axis=0, keepdims=True
    )
    put_row, put_col = count((ROWS, CAP), 0), count((ROWS, CAP), 1)
    put = one_if(put_row == put_col + BLOCK * kept_total) * one_if(put_col < BLOCK * in_len)
    incoming = dot(put.astype(BF16), za[3](source_of(here)))
    att[...] = (attx[:ROWS, :].astype(F32) + incoming).astype(BF16)
    for n in range(NT):
        pout[n] = dot(att[...], wo[:, n * NARROW : (n + 1) * NARROW]).astype(BF16)
    outs[0]()
    z_sum(0)
    z_sum(1)
    outs[1]()
    stores = []

    def keep(src, dst):
        cp = pltpu.make_async_copy(src, dst, store.at[len(stores)])
        cp.start()
        stores.append(cp)

    def keep_piece(chunk, k):
        rows = pl.ds(pl.multiple_of(xat(NX - k) * 256, 256), 256)
        keep(full.at[chunk, rows], sum_o.at[chunk, rows])

    back[2](gtok)
    keep(gtok, gtok_o)
    spread_x(0)
    spread_x(1)
    outs[2](lay)
    keep(lay, lay_o)
    for s in range(2):
        spread_core(s)
        for k in range(NX):
            keep_piece(mine[s], k)
    for s in range(2):
        for k in (0, 1, 3, 2):
            cb_wait(s, k)
            keep_piece(other[s], k)

    for cp in pending:
        cp.wait_send()
    for s in range(2):
        each_z(lambda k: zr_msg(s, k).wait_send())
        each_z(lambda k: zb_msg(s, k).wait_send())
    for cp in stores:
        cp.wait()


def finish(
    lay_i, gtok_i, sum_i, lay_o, gtok_o, giw_o, gow_o, low, wide, flat, lay, gtok, sem_i, sem_o
):
    reads = [pltpu.make_async_copy(sum_i.at[j], low.at[j], sem_i.at[j]) for j in range(4)]
    reads.append(pltpu.make_async_copy(lay_i, lay, sem_i.at[4]))
    reads.append(pltpu.make_async_copy(gtok_i, gtok, sem_i.at[5]))
    copies = []
    for cp in reads:
        cp.start()
    for j in range(3):
        reads[j].wait()
        wide[j] = low[j].astype(F32)
        copies.append(pltpu.make_async_copy(wide.at[j], giw_o.at[j], sem_o.at[j]))
        copies[-1].start()
    reads[3].wait()
    for n in range(NT):
        columns = slice(n * NARROW, (n + 1) * NARROW)
        flat[:, columns] = low[3, columns, :].astype(F32)
    copies.append(pltpu.make_async_copy(flat, gow_o, sem_o.at[3]))
    copies[-1].start()
    for j, src, dst in ((4, lay, lay_o), (5, gtok, gtok_o)):
        reads[j].wait()
        copies.append(pltpu.make_async_copy(src, dst, sem_o.at[j]))
        copies[-1].start()
    for cp in copies:
        cp.wait()


def on_device(tokens, input_weight, output_weight, grad_layer, patch_blocks, target_group):
    vmem = pl.BlockSpec(memory_space=pltpu.VMEM)
    hbm = pl.BlockSpec(memory_space=pl.ANY)
    dma = pltpu.SemaphoreType.DMA

    def buf(*shape, dtype=BF16):
        return pltpu.VMEM(shape, dtype)

    rows_bf16 = jax.ShapeDtypeStruct((ROWS, NARROW), BF16)
    layer_out, grad_tokens, sums = pl.pallas_call(
        kernel,
        out_shape=(rows_bf16, rows_bf16, jax.ShapeDtypeStruct((4, NT * NARROW, NARROW), BF16)),
        in_specs=[hbm] * 4 + [vmem] * 2,
        out_specs=(hbm,) * 3,
        scratch_shapes=[
            buf(3, 1024, NARROW),
            buf(NARROW, 1024),
            buf(NT, ROWS, NARROW),
            buf(NT, NARROW, ROWS),
            buf(NT, EXTRA, NARROW),
            buf(NZ, CAP, NARROW),
            buf(NZ, CAP, NARROW),
            buf(2, CAP, NARROW),
            buf(2, CAP, NARROW),
            buf(ROWS, EXTRA),
            buf(3, ROWS, NARROW),
            buf(ROWS, NARROW),
            buf(ROWS, NARROW),
            buf(3, 2 * CAP, 2 * CAP, dtype=F32),
            buf(ROWS, NARROW),
            buf(EXTRA, NARROW),
            buf(ROWS, 3 * NARROW),
            buf(2, ROWS, NARROW, dtype=F32),
            buf(ROWS, 3 * NARROW, dtype=F32),
            buf(ROWS, NARROW, dtype=F32),
            buf(NT, NARROW, NARROW, dtype=F32),
            buf(3, 1024, NARROW, dtype=F32),
            buf(3, CAP, NARROW),
            buf(NT, NARROW, CAP),
            buf(2 * CAP, CAP, dtype=F32),
            buf(CAP, 3 * NARROW),
            buf(ROWS, NARROW),
            buf(ROWS, NARROW),
            buf(4, 1024, NARROW),
            buf(2, 1024, NARROW),
            buf(2, 1024, NARROW),
            buf(2, 3, 256, NARROW),
            buf(2, 256, NARROW),
            buf(2, NZ, 16, NARROW),
            buf(4, 1024, NARROW),
            buf(NT, ROWS, NARROW),
            buf(NT, ROWS, NARROW),
            buf(7, ROWS, NARROW),
            buf(7, ROWS, NARROW),
            dma((32,)), dma((32,)),
            dma((NT,)), dma((NT,)),
            dma((NZ + 1,)), dma((NZ + 1,)),
            dma((NZ + 1,)), dma((NZ + 1,)),
            dma((2,)), dma((2,)),
            dma((4,)), dma((18,)),
            dma((2,)), dma((2,)),
            dma((2, NX)), dma((2, NX)),
            dma((2, NZ)), dma((2, NZ)),
            dma((2, NZ)), dma((2, NZ)),
            dma((2, NX)), dma((2, NX)),
            dma((2, NX)), dma((2, NX)),
            dma((16,)), dma((16,)),
        ],
        compiler_params=pltpu.CompilerParams(
            collective_id=0, has_side_effects=True, vmem_limit_bytes=56 * 2**20
        ),
    )(
        tokens,
        jnp.transpose(input_weight, (1, 0, 2)),
        output_weight,
        grad_layer,
        patch_blocks.T,
        target_group.T,
    )
    layer_out, grad_tokens, input_sum, output_sum = pl.pallas_call(
        finish,
        out_shape=(
            rows_bf16,
            rows_bf16,
            jax.ShapeDtypeStruct((3, NT * NARROW, NARROW), F32),
            jax.ShapeDtypeStruct((NARROW, NT * NARROW), F32),
        ),
        in_specs=[hbm] * 3,
        out_specs=(hbm,) * 4,
        scratch_shapes=[
            buf(4, NT * NARROW, NARROW),
            buf(3, NT * NARROW, NARROW, dtype=F32),
            buf(NARROW, NT * NARROW, dtype=F32),
            buf(ROWS, NARROW),
            buf(ROWS, NARROW),
            dma((6,)),
            dma((6,)),
        ],
        compiler_params=pltpu.CompilerParams(vmem_limit_bytes=56 * 2**20),
    )(layer_out, grad_tokens, sums)
    return layer_out, grad_tokens, jnp.transpose(input_sum, (1, 0, 2)), output_sum


def solution(mesh):
    return jax.shard_map(
        on_device,
        mesh=mesh,
        in_specs=(
            P(("outer", "dp"), "tensor"),
            P(None, None, "tensor"),
            P("tensor", None),
            P(("outer", "dp"), "tensor"),
            P(),
            P(),
        ),
        out_specs=(
            P(("outer", "dp"), "tensor"),
            P(("outer", "dp"), "tensor"),
            P(None, None, "tensor"),
            P("tensor", None),
        ),
        check_vma=False,
    )
```
